32 devices in a mesh: replica: 1, expert: 32 (over z, y, x, core).
Axes of the slice: x: 2, y: 2, z: 4, core: 2. Of those that a mesh axis runs over, the one named last changes fastest.
Arguments:
- hidden_states: bfloat16 [4, 448, 4096], P(None, ('replica', 'expert')), may hold values from -6 to 6
- routes: int32 [4, 448, 8], P(None, ('replica', 'expert')), may hold values from 0 to 63, all different within a row; in each aligned block of 14 rows (0 to 13, 14 to 27, ..., all dimensions but the last counted through in order) at most 3 rows name the same one
- gates: float32 [4, 448, 8], P(None, ('replica', 'expert')), may hold values from 0.05 to 1
- w_gate: bfloat16 [64, 4096, 768], P('expert', 'replica'), may hold values from -0.09375 to 0.09375
- w_up: bfloat16 [64, 4096, 768], P('expert', 'replica'), may hold values from -0.09375 to 0.09375
- queries: bfloat16 [4, 448, 8192], P(None, ('replica', 'expert')), may hold values from -200 to 200
- new_keys: bfloat16 [4, 448, 512], P(None, ('replica', 'expert')), may hold values from -6 to 6
- new_values: bfloat16 [4, 448, 512], P(None, ('replica', 'expert')), may hold values from -6 to 6
- cache_keys: bfloat16 [448, 128, 512], P(('replica', 'expert')), may hold values from -6 to 6
- cache_values: bfloat16 [448, 128, 512], P(('replica', 'expert')), may hold values from -6 to 6
- lengths: int32 [448], P(('replica', 'expert')), may hold values from 2 to 128, as said below
Outputs:
- moe_hidden: bfloat16 [4, 448, 6144], P(None, ('replica', 'expert'))
- attn_out: bfloat16 [4, 448, 8192], P(None, ('replica', 'expert'))
The draws below stay inside these ranges and needn't reach their ends.
Inputs may be any that keep to these rules, and one draw needn't show every extreme that they name: `routes`: each token names 8 different experts; among the 14 tokens of one device at one step no expert is named more than 3 times, and in some such blocks one expert is named exactly 3 times. `lengths`: some rollout holds exactly 128 cached entries.
All inputs are finite; a program needn't handle non-finite values.
Results may differ from the reference program's by a relative error of at most 0.0065.
Values may be sent and summed in bfloat16 or wider, within the bound.
No kernel may reach another device: no remote copies, remote signals or barrier semaphores. Data moves between devices by JAX's collectives and lax.ppermute only.
A program may use at most 128 MiB of HBM per device.

```python
import math
import jax
import jax.numpy as jnp
import numpy as np
from jax import lax

D = 4096
FH = 768
HQ = 64
KVH = 4
HD = 128
TOPK = 8
STEPS = 4
ROLL_DEV = 14
CACHE_LEN = 128
EXPERTS = 64
CAP = 3
TOKENS = 448


def lengths_from(key):
    drawn = jax.random.randint(jax.random.fold_in(key, 11), (TOKENS,), 2, CACHE_LEN + 1)
    picked = jax.random.randint(jax.random.fold_in(key, 12), (), 0, TOKENS)
    return jnp.where(jnp.arange(TOKENS) == picked, CACHE_LEN, drawn).astype(jnp.int32)


def draw_lengths(key, part):
    return lengths_from(key)


def draw_cache_keys(key, part):
    base = jnp.clip(jax.random.normal(jax.random.fold_in(key, 21), (TOKENS, CACHE_LEN, KVH, HD), jnp.float32), -6.0, 6.0)
    return base.reshape(TOKENS, CACHE_LEN, KVH * HD).astype(jnp.bfloat16)


def draw_queries(key, part):
    groups = HQ // KVH
    base = jnp.clip(jax.random.normal(jax.random.fold_in(key, 31), (STEPS, TOKENS, KVH, groups, HD), jnp.float32), -6.0, 6.0)
    return base.reshape(STEPS, TOKENS, HQ * HD).astype(jnp.bfloat16)


def block_levels(key, extent, shards, least, top_value):
    level, own = 1.0, jax.random.fold_in(key, 6)
    for position, shards_of in shards:
        draws = jnp.exp(jax.random.uniform(jax.random.fold_in(own, position), (shards_of,), jnp.float32, least / len(shards), top_value / len(shards)))
        level = level * jnp.repeat(draws, extent[position] // shards_of).reshape([-1 if axis == position else 1 for axis in range(len(extent))])
    return level


def assign_block(key, own, number, rows, number_of, top, bound, slope):
    ranking = jax.random.permutation(key, number_of)
    heavy_load, common = load_shares(number_of, rows * top, bound, slope, True), load_shares(number_of, rows * top, bound, slope, False)
    places = jnp.arange(number_of)

    def named(tallies, offset_by):
        used = int((tallies > 0).sum())
        fixed = max(1, used // 4)
        moved = fixed + (places - fixed + offset_by * (used - fixed)) % max(1, number_of - fixed)
        return jnp.zeros((number_of,), jnp.int32).at[ranking[jnp.where(places < fixed, places, moved)]].set(jnp.asarray(tallies, jnp.int32))

    tallies = jnp.where(number % 4 == 0, named(heavy_load, number // 4), named(common, number - number // 4 - 1))
    mixed = jax.random.permutation(jax.random.fold_in(own, 3), number_of)
    source_of, taker = mixed[0:number_of // 2 * 2:2], mixed[1:number_of // 2 * 2:2]
    room = jnp.minimum(tallies[source_of] - 1, bound - tallies[taker]) // 2
    room = jnp.where((source_of == ranking[0]) | (taker == ranking[0]) | (tallies[taker] == 0), 0, jnp.maximum(room, 0))
    moved = jax.random.randint(jax.random.fold_in(own, 4), (number_of // 2,), 0, 1 << 20) % (room + 1)
    tallies = tallies.at[source_of].add(-moved).at[taker].add(moved)
    items = jnp.searchsorted(jnp.cumsum(tallies), jnp.arange(rows * top), side="right").astype(jnp.int32)
    table = items.reshape(top, rows).T
    table = table[jax.random.permutation(jax.random.fold_in(own, 1), rows)]
    offset_by = jax.random.randint(jax.random.fold_in(own, 2), (rows, 1), 0, top)
    return jnp.take_along_axis(table, (jnp.arange(top)[None, :] + offset_by) % top, axis=1)


def load_shares(count, total, most, slope, full):
    weights = [(1 << 20) // math.isqrt(rank ** slope) + 1 for rank in range(1, count + 1)]
    largest = most if full else min(most, max(-(-total // count), total * weights[0] // sum(weights)))
    least = 1 if total - largest >= count - 1 else 0
    given, surplus = [largest] + [least] * (count - 1), total - largest - least * (count - 1)
    while surplus > 0:
        free = [i for i in range(1, count) if given[i] < largest] or [i for i in range(1, count) if given[i] < most]
        mass, left = sum([weights[i] for i in free]), surplus
        for i in free:
            more = min(most - given[i], max(1, left * weights[i] // mass), surplus)
            given[i] = given[i] + more
            surplus = surplus - more
    return np.array(given)


def noise(stream_key, shape, scale, bound, pieces=(), kind=jnp.bfloat16):
    entries = scale * jax.random.normal(stream_key, shape, jnp.float32)
    if pieces:
        entries = entries * block_levels(stream_key, shape, pieces, -0.22, 0.18)
    return jnp.clip(entries, -bound, bound).astype(kind)


def setup_inputs(seed: int = 0) -> dict:
    streams_of = jax.random.split(jax.random.key(seed), 12)
    hidden_states = noise(streams_of[0], (STEPS, TOKENS, D), 1.0, 6.0, ((1, 32),))
    routes_keys = jax.random.split(jax.random.fold_in(streams_of[1], 1), STEPS * TOKENS // ROLL_DEV)
    routes_turns = jax.random.permutation(jax.random.fold_in(streams_of[1], 3), STEPS * TOKENS // ROLL_DEV)
    routes = jax.vmap(lambda own, number: assign_block(jax.random.fold_in(streams_of[1], 2), own, number, ROLL_DEV, EXPERTS, TOPK, CAP, 2))(routes_keys, routes_turns).reshape((STEPS, TOKENS, TOPK))
    gates = jnp.clip(jnp.exp(math.log(1.0) - 2.9957323 * jax.random.uniform(streams_of[2], (STEPS, TOKENS, TOPK), jnp.float32) ** block_levels(streams_of[2], (STEPS, TOKENS, TOPK), ((1, 32),), -0.2, 0.2)), 0.05, 1.0)
    w_gate = noise(streams_of[3], (EXPERTS, D, FH), D ** -0.5, 0.09375, ((0, 32),))
    w_up = noise(streams_of[4], (EXPERTS, D, FH), D ** -0.5, 0.09375, ((0, 32),))
    queries = draw_queries(jax.random.fold_in(streams_of[11], 71), 0)
    new_keys = noise(streams_of[6], (STEPS, TOKENS, KVH * HD), 1.0, 6.0, ((1, 32),))
    new_values = noise(streams_of[7], (STEPS, TOKENS, KVH * HD), 1.0, 6.0, ((1, 32),))
    cache_keys = draw_cache_keys(jax.random.fold_in(streams_of[11], 71), 0)
    cache_values = noise(streams_of[9], (TOKENS, CACHE_LEN, KVH * HD), 1.0, 6.0, ((0, 32),))
    lengths = draw_lengths(jax.random.fold_in(streams_of[11], 71), 0)
    return dict(hidden_states=hidden_states, routes=routes, gates=gates, w_gate=w_gate, w_up=w_up, queries=queries, new_keys=new_keys, new_values=new_values, cache_keys=cache_keys, cache_values=cache_values, lengths=lengths)


def attend_block(queried, keys_cached, values_cached, keys_new, values_new, lens_block):
    groups = HQ // KVH
    rows_here = keys_cached.shape[0]
    query_f = queried.reshape(STEPS, rows_here, KVH, groups, HD).astype(jnp.float32)
    kc_f = keys_cached.reshape(rows_here, CACHE_LEN, KVH, HD).astype(jnp.float32)
    vc_f = values_cached.reshape(rows_here, CACHE_LEN, KVH, HD).astype(jnp.float32)
    kn_f = keys_new.reshape(STEPS, rows_here, KVH, HD).astype(jnp.float32)
    vn_f = values_new.reshape(STEPS, rows_here, KVH, HD).astype(jnp.float32)
    score_scale = 1.0 / math.sqrt(HD)
    valid_cache = (jnp.arange(CACHE_LEN, dtype=jnp.int32)[None, :] < lens_block[:, None])[None, :, None, None, :]
    valid_new = (jnp.arange(STEPS, dtype=jnp.int32)[None, :] <= jnp.arange(STEPS, dtype=jnp.int32)[:, None])[:, None, None, None, :]
    scores_cache = jnp.einsum('srghd,rlgd->srghl', query_f, kc_f) * score_scale
    scores_cache = jnp.where(valid_cache, scores_cache, -jnp.inf)
    scores_new = jnp.einsum('srghd,jrgd->srghj', query_f, kn_f) * score_scale
    scores_new = jnp.where(valid_new, scores_new, -jnp.inf)
    top_score = jnp.maximum(lax.optimization_barrier(jnp.max(scores_cache, axis=-1, keepdims=True)), lax.optimization_barrier(jnp.max(scores_new, axis=-1, keepdims=True)))
    weights_cache = jnp.exp(scores_cache - top_score)
    weights_new = jnp.exp(scores_new - top_score)
    total_weight = lax.optimization_barrier(jnp.sum(weights_cache, axis=-1, keepdims=True)) + lax.optimization_barrier(jnp.sum(weights_new, axis=-1, keepdims=True))
    probs_cache = (weights_cache / total_weight).astype(jnp.bfloat16).astype(jnp.float32)
    probs_new = (weights_new / total_weight).astype(jnp.bfloat16).astype(jnp.float32)
    attended = jnp.einsum('srghl,rlgd->srghd', probs_cache, vc_f) + jnp.einsum('srghj,jrgd->srghd', probs_new, vn_f)
    return attended.astype(jnp.bfloat16).reshape(STEPS, rows_here, HQ * HD)

def reference(hidden_states, routes, gates, w_gate, w_up, queries, new_keys, new_values, cache_keys, cache_values, lengths):
    states_f32 = hidden_states.astype(jnp.float32)
    normed = (states_f32 * lax.rsqrt(lax.optimization_barrier(jnp.mean(states_f32 * states_f32, axis=-1, keepdims=True)) + 1e-06)).astype(jnp.bfloat16)
    mixing = gates / lax.optimization_barrier(jnp.sum(gates, axis=-1, keepdims=True))
    blocks = TOKENS // ROLL_DEV
    pair_count = ROLL_DEV * TOPK
    route_pairs = routes.reshape(STEPS, blocks, pair_count)
    mixing_pairs = mixing.reshape(STEPS, blocks, pair_count)
    onehot = (route_pairs[..., None] == jnp.arange(EXPERTS, dtype=jnp.int32)).astype(jnp.int32)
    earlier = jnp.cumsum(onehot, axis=2) - onehot
    slot_ids = lax.optimization_barrier(jnp.sum(earlier * onehot, axis=-1)).astype(jnp.int32)
    pair_numbers = jnp.broadcast_to(jnp.arange(pair_count, dtype=jnp.int32)[None, None, :], route_pairs.shape)
    normed_blocks = normed.reshape(STEPS, blocks, ROLL_DEV, D)
    step_index = jnp.arange(STEPS, dtype=jnp.int32)[:, None, None]
    block_index = jnp.arange(blocks, dtype=jnp.int32)[None, :, None]

    def one_expert(total, stuff):
        expert_id, gate_mat, up_mat = stuff
        chosen = route_pairs == expert_id
        where_slot = jnp.where(chosen, slot_ids, CAP).astype(jnp.int32)
        pair_of_slot = jnp.zeros((STEPS, blocks, CAP + 1), jnp.int32).at[step_index, block_index, where_slot].set(pair_numbers)[..., :CAP]
        filled = jnp.zeros((STEPS, blocks, CAP + 1), jnp.float32).at[step_index, block_index, where_slot].set(1.0)[..., :CAP]
        token_of_slot = (pair_of_slot // TOPK).astype(jnp.int32)
        rows = normed_blocks[step_index, block_index, token_of_slot]
        flat_rows = rows.reshape(-1, D)
        gate_act = jnp.dot(flat_rows, gate_mat, preferred_element_type=jnp.float32)
        up_act = jnp.dot(flat_rows, up_mat, preferred_element_type=jnp.float32)
        inner_act = (jax.nn.silu(gate_act) * up_act).astype(jnp.bfloat16)
        inner_act = inner_act.reshape(STEPS, blocks, CAP, FH).astype(jnp.float32)
        total = total.at[step_index, block_index, pair_of_slot].add(filled[..., None] * inner_act)
        return (total, None)
    start_total = jnp.zeros((STEPS, blocks, pair_count, FH), jnp.float32)
    total, _ = lax.scan(one_expert, start_total, (jnp.arange(EXPERTS, dtype=jnp.int32), w_gate, w_up))
    moe_hidden = (total * mixing_pairs[..., None]).reshape(STEPS, TOKENS, TOPK * FH).astype(jnp.bfloat16)

    def per_block(stuff):
        return attend_block(*stuff)
    query_blocks = jnp.moveaxis(queries.reshape(STEPS, blocks, ROLL_DEV, HQ * HD), 1, 0)
    kn_blocks = jnp.moveaxis(new_keys.reshape(STEPS, blocks, ROLL_DEV, KVH * HD), 1, 0)
    vn_blocks = jnp.moveaxis(new_values.reshape(STEPS, blocks, ROLL_DEV, KVH * HD), 1, 0)
    kc_blocks = cache_keys.reshape(blocks, ROLL_DEV, CACHE_LEN, KVH * HD)
    vc_blocks = cache_values.reshape(blocks, ROLL_DEV, CACHE_LEN, KVH * HD)
    len_blocks = lengths.reshape(blocks, ROLL_DEV)
    attended = lax.map(per_block, (query_blocks, kc_blocks, vc_blocks, kn_blocks, vn_blocks, len_blocks))
    attn_out = jnp.moveaxis(attended, 0, 1).reshape(STEPS, TOKENS, HQ * HD)
    return (moe_hidden, attn_out)
```

```python
import math

import jax
import jax.numpy as jnp
import numpy as np
from jax import lax
from jax.experimental import pallas as pl
from jax.experimental.pallas import tpu as pltpu
from jax.sharding import PartitionSpec as P

HQ = 64
KVH = 4
HD = 128
TOPK = 8
LANES = 128
EDGE = 2
INNER = EDGE**3
VMEM_BYTES = 48 * 1024 * 1024


def attention(queries, new_keys, new_values, cache_keys, cache_values, lengths):
    steps_total, local_rows, _ = queries.shape
    groups = HQ // KVH
    queried = queries.reshape(steps_total, local_rows, KVH, groups, HD)
    cache_len = cache_keys.shape[1]
    keys_cached = cache_keys.reshape(local_rows, cache_len, KVH, HD)
    values_cached = cache_values.reshape(local_rows, cache_len, KVH, HD)
    keys_new = new_keys.reshape(steps_total, local_rows, KVH, HD)
    values_new = new_values.reshape(steps_total, local_rows, KVH, HD)
    score_scale = 1.0 / math.sqrt(HD)
    valid_cache = (jnp.arange(cache_len, dtype=jnp.int32)[None, :] < lengths[:, None])[
        None, :, None, None, :
    ]
    valid_new = (
        jnp.arange(steps_total, dtype=jnp.int32)[None, :]
        <= jnp.arange(steps_total, dtype=jnp.int32)[:, None]
    )[:, None, None, None, :]
    scores_cache = (
        jnp.einsum("srghd,rlgd->srghl", queried, keys_cached, preferred_element_type=jnp.float32)
        * score_scale
    )
    scores_cache = jnp.where(valid_cache, scores_cache, -jnp.inf)
    scores_new = (
        jnp.einsum("srghd,jrgd->srghj", queried, keys_new, preferred_element_type=jnp.float32)
        * score_scale
    )
    scores_new = jnp.where(valid_new, scores_new, -jnp.inf)
    top_score = jnp.maximum(
        jnp.max(scores_cache, axis=-1, keepdims=True), jnp.max(scores_new, axis=-1, keepdims=True)
    )
    weights_cache = jnp.exp(scores_cache - top_score)
    weights_new = jnp.exp(scores_new - top_score)
    total_weight = jnp.sum(weights_cache, axis=-1, keepdims=True) + jnp.sum(
        weights_new, axis=-1, keepdims=True
    )
    probs_cache = (weights_cache / total_weight).astype(jnp.bfloat16)
    probs_new = (weights_new / total_weight).astype(jnp.bfloat16)
    attended = jnp.einsum(
        "srghl,rlgd->srghd", probs_cache, values_cached, preferred_element_type=jnp.float32
    )
    attended = attended + jnp.einsum(
        "srghj,jrgd->srghd", probs_new, values_new, preferred_element_type=jnp.float32
    )
    return attended.astype(jnp.bfloat16).reshape(steps_total, local_rows, HQ * HD)


def place(index):
    return index // INNER, index // 4 % EDGE, index // 2 % EDGE, index % EDGE


def device_at(line, row, column, side):
    return ((line * EDGE + row) * EDGE + column) * EDGE + side


def moves(peers, target):
    return [(index, device_at(*target(*place(index)))) for index in range(peers)]


def padded(rows):
    return -(-rows // 16) * 16


def prepare_kernel(states_ref, routes_ref, order_ref, payload_ref, *, capacity, experts):
    width = states_ref.shape[1]
    states = states_ref[...].astype(jnp.float32)
    scale = lax.rsqrt(jnp.mean(states * states, axis=-1, keepdims=True) + 1e-06)
    payload_ref[:, :width] = (states * scale).astype(payload_ref.dtype)
    routes = routes_ref[...]
    rows = routes.shape[0]
    expert_ids = lax.broadcasted_iota(jnp.int32, (rows, experts), 1)
    marks = [
        (routes[:, choice : choice + 1] == expert_ids).astype(jnp.float32)
        for choice in range(TOPK)
    ]
    named = sum(marks)
    earlier = jnp.dot(
        order_ref[...], named.astype(jnp.bfloat16), preferred_element_type=jnp.float32
    )
    lane_ids = lax.broadcasted_iota(jnp.int32, (rows, LANES), 1)
    codes = jnp.full((rows, LANES), -1.0, jnp.float32)
    for choice in range(TOPK):
        slot = jnp.sum(earlier * marks[choice], axis=-1, keepdims=True)
        expert = routes[:, choice : choice + 1].astype(jnp.float32)
        codes = jnp.where(lane_ids == choice, expert, codes)
        codes = jnp.where(lane_ids == TOPK + choice, slot, codes)
    payload_ref[:, width:] = codes.astype(payload_ref.dtype)


def prepare(states, routes, steps_total, capacity, experts):
    rows, width = states.shape
    local_rows = rows // steps_total
    numbers = np.arange(rows)
    order = (numbers[:, None] // local_rows == numbers[None, :] // local_rows) & (
        numbers[:, None] > numbers[None, :]
    )
    return pl.pallas_call(
        lambda *refs: prepare_kernel(*refs, capacity=capacity, experts=experts),
        out_shape=jax.ShapeDtypeStruct((rows, width + LANES), jnp.bfloat16),
        compiler_params=pltpu.CompilerParams(vmem_limit_bytes=VMEM_BYTES),
        name="prepare",
    )(states, routes, jnp.asarray(order, jnp.bfloat16))


def pick_kernel(own_ref, near_ref, far_ref, same_ref, expert_ref, slot_ref, keep_ref, send_ref):
    width = keep_ref.shape[1]
    rows = jnp.concatenate([own_ref[...], near_ref[...], far_ref[...]], axis=0)
    codes = rows[:, width:].astype(jnp.float32)
    wanted_expert, wanted_slot = expert_ref[...], slot_ref[...]
    hits = jnp.zeros((rows.shape[0], wanted_expert.shape[1]), jnp.float32)
    for choice in range(TOPK):
        match = (codes[:, choice : choice + 1] == wanted_expert) & (
            codes[:, TOPK + choice : TOPK + choice + 1] == wanted_slot
        )
        hits = jnp.where(match, 1.0, hits)
    onehot = (hits * same_ref[...]).astype(jnp.bfloat16)
    kept = keep_ref.shape[0]
    picked = lax.dot_general(
        onehot,
        rows[:, :width],
        (((0,), (0,)), ((), ())),
        preferred_element_type=jnp.float32,
    ).astype(keep_ref.dtype)
    keep_ref[...] = picked[:kept]
    send_ref[...] = picked[kept:]


def slot_tables(steps_total, local_rows, capacity, experts_local):
    entries = []
    for side, blocks in ((0, (0, 1, 2, 3, 4)), (1, (2, 3, 4))):
        for expert in range(experts_local):
            group = [
                (side, expert, block, step, slot)
                for block in blocks
                for step in range(steps_total)
                for slot in range(capacity)
            ]
            entries += group + [(side, expert, -1, -1, -1)] * (padded(len(group)) - len(group))
    return np.array(entries, np.int32)


def expert_kernel(*refs, pairs, kept, sent):
    x_refs, (gate_ref, up_ref, out_ref, rows_ref) = refs[: 2 * pairs], refs[2 * pairs :]

    @pl.when(pl.program_id(1) == 0)
    def _():
        expert, at = pl.program_id(0), 0
        for number, x_ref in enumerate(x_refs):
            part = sent if number % 2 else kept
            rows_ref[at : at + part, :] = x_ref[pl.ds(pl.multiple_of(expert * part, 16), part), :]
            at += part

    rows = rows_ref[...]
    gate = jnp.dot(rows, gate_ref[0], preferred_element_type=jnp.float32)
    up = jnp.dot(rows, up_ref[0], preferred_element_type=jnp.float32)
    out_ref[0] = (gate / (1.0 + jnp.exp(-gate)) * up).astype(out_ref.dtype)


def run_experts(arrays, w_gate, w_up):
    experts_local, width, hidden = w_gate.shape
    kept, sent = arrays[0].shape[0] // experts_local, arrays[1].shape[0] // experts_local
    pairs = len(arrays) // 2
    rows = pairs * (kept + sent)
    block = 2 * LANES
    return pl.pallas_call(
        lambda *refs: expert_kernel(*refs, pairs=pairs, kept=kept, sent=sent),
        grid=(experts_local, hidden // block),
        in_specs=[pl.BlockSpec(a.shape, lambda e, f: (0, 0)) for a in arrays]
        + [pl.BlockSpec((1, width, block), lambda e, f: (e, 0, f))] * 2,
        out_specs=pl.BlockSpec((1, rows, block), lambda e, f: (e, 0, f)),
        out_shape=jax.ShapeDtypeStruct((experts_local, rows, hidden), jnp.bfloat16),
        scratch_shapes=[pltpu.VMEM((rows, width), jnp.bfloat16)],
        compiler_params=pltpu.CompilerParams(vmem_limit_bytes=VMEM_BYTES),
        cost_estimate=pl.CostEstimate(
            flops=4 * experts_local * rows * width * hidden,
            bytes_accessed=4 * experts_local * width * hidden,
            transcendentals=experts_local * rows * hidden,
        ),
        name="experts",
    )(*arrays, w_gate, w_up)


def per_device(
    hidden_states,
    routes,
    gates,
    w_gate,
    w_up,
    queries,
    new_keys,
    new_values,
    cache_keys,
    cache_values,
    lengths,
):
    peers = lax.axis_size("expert")
    me = lax.axis_index("expert")
    lines = peers // INNER
    experts_local = w_gate.shape[0]
    experts = experts_local * peers
    steps_total, local_rows, model_width = hidden_states.shape
    capacity = local_rows * TOPK * 2 // experts
    slot_span = steps_total * capacity
    gate_full, up_full = (
        lax.all_gather(w_gate, "replica", axis=1, tiled=True),
        lax.all_gather(w_up, "replica", axis=1, tiled=True),
    )
    hidden_width = gate_full.shape[2]
    block_rows = steps_total * local_rows

    send = lambda array, target: lax.ppermute(array, "expert", moves(peers, target))
    to_line = lambda offset: lambda z, y, x, c: (z ^ offset, y, x, c)
    first_hop = lambda z, y, x, c: (z, y ^ c, x ^ (1 - c), c)
    second_hop = lambda z, y, x, c: (z, y ^ (1 - c), x ^ c, c)
    other_side = lambda z, y, x, c: (z, y, x, 1 - c)
    sides = [[EDGE * chip + side for side in range(EDGE)] for chip in range(peers // EDGE)]
    z, y, x, side = place(me)

    payload = prepare(
        hidden_states.reshape(block_rows, model_width),
        routes.reshape(block_rows, TOPK),
        steps_total,
        capacity,
        experts,
    )
    tables = slot_tables(steps_total, local_rows, capacity, experts_local)
    kept_rows = int((tables[:, 0] == 0).sum())
    token_block = np.arange(5 * block_rows) // block_rows
    token_step = np.arange(5 * block_rows) % block_rows // local_rows
    same = (token_block[:, None] == tables[None, :, 2]) & (token_step[:, None] == tables[None, :, 3])
    wanted_expert = (
        jnp.where(tables[:, 0] == 0, me, me ^ 1) * experts_local + tables[:, 1]
    ).astype(jnp.float32)[None]
    wanted_slot = jnp.asarray(tables[:, 4], jnp.float32)[None]
    pick = pl.pallas_call(
        pick_kernel,
        out_shape=(
            jax.ShapeDtypeStruct((kept_rows, model_width), jnp.bfloat16),
            jax.ShapeDtypeStruct((len(tables) - kept_rows, model_width), jnp.bfloat16),
        ),
        compiler_params=pltpu.CompilerParams(vmem_limit_bytes=VMEM_BYTES),
        name="pick",
    )

    arrived, last = [payload], payload
    for offset in range(1, lines):
        source = payload
        if offset > 2:
            source, last = lax.optimization_barrier((payload, last))
            arrived[-1] = last
        last = send(source, to_line(offset))
        arrived.append(last)
    blocks = []
    for own in arrived:
        pair = lax.all_gather(own, "expert", axis_index_groups=sides, tiled=True)
        near = send(pair, first_hop)
        half = lax.dynamic_slice_in_dim(near, side * block_rows, block_rows)
        far = send(half, second_hop)
        keep, give = pick(
            pair, near, far, jnp.asarray(same, jnp.float32), wanted_expert, wanted_slot
        )
        blocks.append((keep, send(give, other_side)))
    inner = []
    batch = max(1, lines // 2)
    for start in range(0, lines, batch):
        arrays = [array for pair in blocks[start : start + batch] for array in pair]
        inner.append(run_experts(arrays, gate_full, up_full))
    kept, sent = kept_rows // experts_local, (len(tables) - kept_rows) // experts_local
    computed = jnp.concatenate([part.reshape(-1, hidden_width) for part in inner], axis=0)
    numbers = jnp.arange(experts * slot_span, dtype=jnp.int32)
    owner, expert, rest = (
        numbers // (experts_local * slot_span),
        numbers // slot_span % experts_local,
        numbers % slot_span,
    )
    oz, oy, ox, oc = place(owner)
    item = oz ^ z
    own_chip, far_chip = (oy == y) & (ox == x), (oy != y) & (ox != x)
    mine = jnp.where(side == 0, oy == y, ox == x)
    kept_block = jnp.where(own_chip, oc, jnp.where(far_chip, 4, 2 + oc))
    sent_block = jnp.where(far_chip, 2, oc)
    kept_here = own_chip | jnp.where(far_chip, oc == side, mine)
    in_item = jnp.where(kept_here, kept_block * slot_span, kept + sent_block * slot_span) + rest
    call = item // batch
    row_of = (
        (call * experts_local + expert) * batch + item % batch
    ) * (kept + sent) + in_item
    row_marks = (row_of[:, None] == jnp.arange(computed.shape[0], dtype=jnp.int32)).astype(
        jnp.bfloat16
    )
    outgoing = jnp.dot(row_marks, computed, preferred_element_type=jnp.float32).astype(jnp.bfloat16)
    outgoing = outgoing.reshape(peers, experts_local * slot_span, hidden_width)
    returned = lax.all_to_all(outgoing, "expert", split_axis=0, concat_axis=0, tiled=True)
    back_rows = returned.reshape(experts * slot_span, hidden_width)

    mixing = gates / jnp.sum(gates, axis=-1, keepdims=True)
    pair_ids = routes.reshape(steps_total, local_rows * TOPK)
    onehot = (pair_ids[..., None] == jnp.arange(experts, dtype=jnp.int32)).astype(jnp.int32)
    earlier = jnp.cumsum(onehot, axis=1) - onehot
    slot_ids = jnp.sum(earlier * onehot, axis=-1).reshape(steps_total, local_rows, TOPK)
    columns = (
        routes * slot_span
        + jnp.arange(steps_total, dtype=jnp.int32)[:, None, None] * capacity
        + slot_ids
    )
    picker = (columns[..., None] == jnp.arange(experts * slot_span, dtype=jnp.int32)).astype(
        jnp.bfloat16
    )
    picked = jnp.einsum("srkc,cf->srkf", picker, back_rows, preferred_element_type=jnp.float32)
    moe_hidden = (
        (picked * mixing[..., None])
        .reshape(steps_total, local_rows, TOPK * hidden_width)
        .astype(jnp.bfloat16)
    )
    attn_out = attention(queries, new_keys, new_values, cache_keys, cache_values, lengths)
    return (moe_hidden, attn_out)


def solution(mesh):
    in_specs = (
        P(None, ("replica", "expert"), None),
        P(None, ("replica", "expert"), None),
        P(None, ("replica", "expert"), None),
        P("expert", "replica", None),
        P("expert", "replica", None),
        P(None, ("replica", "expert"), None),
        P(None, ("replica", "expert"), None),
        P(None, ("replica", "expert"), None),
        P(("replica", "expert"), None, None),
        P(("replica", "expert"), None, None),
        P(("replica", "expert")),
    )
    out_specs = (P(None, ("replica", "expert"), None), P(None, ("replica", "expert"), None))
    return jax.shard_map(
        per_device, mesh=mesh, in_specs=in_specs, out_specs=out_specs, check_vma=False
    )
```

```python
import functools
import math

import jax
import jax.numpy as jnp
import numpy as np
from jax import lax
from jax.experimental import pallas as pl
from jax.experimental.pallas import tpu as pltpu
from jax.sharding import PartitionSpec as P

HQ = 64
KVH = 4
HD = 128
TOPK = 8
LANES = 128
EDGE = 2
INNER = EDGE**3
VMEM_BYTES = 60 * 1024 * 1024


def attention_kernel(lengths_ref, q_ref, nk_ref, nv_ref, k_ref, v_ref, out_ref, *, groups):
    rows, steps, _ = q_ref.shape
    cache = k_ref.shape[1]
    extra = 16
    many = steps*groups
    scale = 1.0/math.sqrt(HD)
    shape = (cache+extra, 2*many)
    position = lax.broadcasted_iota(jnp.int32, shape, 0)
    step = lax.broadcasted_iota(jnp.int32, shape, 1) % steps
    first = pl.program_id(0)*rows
    pad = jnp.zeros((extra-steps, 2*HD), jnp.float32)
    none = jnp.zeros((many, HD), jnp.float32)
    for r in range(rows):
        limit = jnp.where(position < cache, lengths_ref[first + r], step + (cache + 1))
        valid = position < limit
        for pair in range(KVH//2):
            wide = pl.ds(pair*2*HD, 2*HD)
            def with_new(cached, new):
                fresh = jnp.concatenate([new[r, :, wide].astype(jnp.float32), pad], axis=0)
                return jnp.concatenate([cached[r, :, wide], fresh.astype(jnp.bfloat16)], axis=0)
            heads = [q_ref[r, :, (pair*2*groups+h)*HD:(pair*2*groups+h+1)*HD].astype(jnp.float32) for h in range(2*groups)]
            low = jnp.concatenate(heads[:groups], axis=0)
            high = jnp.concatenate(heads[groups:], axis=0)
            asked = jnp.concatenate([jnp.concatenate([low, none], axis=1), jnp.concatenate([none, high], axis=1)], axis=0).astype(jnp.bfloat16)
            scores = lax.dot_general(with_new(k_ref, nk_ref), asked, (((1,),(1,)),((),())), preferred_element_type=jnp.float32)*scale
            scores = jnp.where(valid, scores, -jnp.inf)
            weights = jnp.exp(scores - jnp.max(scores, axis=0, keepdims=True))
            probs = (weights * (1.0/jnp.sum(weights, axis=0, keepdims=True))).astype(jnp.bfloat16)
            mixed = lax.dot_general(probs, with_new(v_ref, nv_ref), (((0,),(0,)),((),())), preferred_element_type=jnp.float32)
            for h in range(2*groups):
                at = h//groups*HD
                out_ref[r, :, (pair*2*groups+h)*HD:(pair*2*groups+h+1)*HD] = mixed[h*steps:(h+1)*steps, at:at+HD].astype(out_ref.dtype)

def attention(queries,new_keys,new_values,cache_keys,cache_values,lengths):
    steps, rows, _ = queries.shape
    groups = HQ//KVH
    cache = cache_keys.shape[1]
    part = max(n for n in range(1,8) if rows % n == 0)
    turn = lambda a: jnp.swapaxes(a,0,1)
    spec = lambda a: pl.BlockSpec((part,)+a.shape[1:], lambda i:(i,0,0))
    arrays = (turn(queries), turn(new_keys), turn(new_values), cache_keys, cache_values)
    out= pl.pallas_call(
        functools.partial(attention_kernel, groups=groups),
        grid=(rows//part,),
        in_specs=[pl.BlockSpec(memory_space=pltpu.SMEM)]+[spec(a) for a in arrays],
        out_specs=spec(arrays[0]),
        out_shape=jax.ShapeDtypeStruct(arrays[0].shape, queries.dtype),
        compiler_params=pltpu.CompilerParams(vmem_limit_bytes=16 * 1024 * 1024),
        name="attention",
    )(lengths, *arrays)
    return turn(out)


def place(index):
    return index // INNER, index // 4 % EDGE, index // 2 % EDGE, index % EDGE


def device_at(line, row, column, side):
    return ((line * EDGE + row) * EDGE + column) * EDGE + side


def moves(peers, target):
    return [(index, device_at(*target(*place(index)))) for index in range(peers)]


def padded(rows):
    return -(-rows // 16) * 16


def prepare_kernel(states_ref, routes_ref, order_ref, payload_ref, columns_ref, *, capacity, experts):
    tokens, steps, width = states_ref.shape
    states = jnp.concatenate(
        [states_ref[token].astype(jnp.float32) for token in range(tokens)], axis=0
    )
    scale = lax.rsqrt(jnp.mean(states * states, axis=-1, keepdims=True) + 1e-06)
    payload_ref[:, :width] = (states * scale).astype(payload_ref.dtype)
    routes = routes_ref[...]
    rows = tokens * steps
    expert_ids = lax.broadcasted_iota(jnp.int32, (rows, experts), 1)
    marks = [
        (routes[:, choice : choice + 1] == expert_ids).astype(jnp.float32)
        for choice in range(TOPK)
    ]
    named = sum(marks)
    earlier = jnp.dot(
        order_ref[...], named.astype(jnp.bfloat16), preferred_element_type=jnp.float32
    )
    lane_ids = lax.broadcasted_iota(jnp.int32, (rows, LANES), 1)
    step = lax.broadcasted_iota(jnp.int32, (rows, 1), 0) % steps
    codes = jnp.zeros((rows, LANES), jnp.float32)
    columns = jnp.zeros((rows, LANES), jnp.int32)
    for choice in range(TOPK):
        slot = jnp.sum(earlier * marks[choice], axis=-1, keepdims=True)
        expert = routes[:, choice : choice + 1]
        code = expert.astype(jnp.float32) * capacity + slot
        codes = jnp.where(lane_ids == choice, code, codes)
        column = (expert * steps + step) * capacity + slot.astype(jnp.int32)
        columns = jnp.where(lane_ids == choice, column, columns)
    payload_ref[:, width:] = codes.astype(payload_ref.dtype)
    columns_ref[...] = columns


def prepare(states, routes, capacity, experts):
    tokens, steps, width = states.shape
    rows = tokens * steps
    numbers = np.arange(rows)
    order = (numbers[:, None] % steps == numbers[None, :] % steps) & (
        numbers[:, None] > numbers[None, :]
    )
    return pl.pallas_call(
        functools.partial(prepare_kernel, capacity=capacity, experts=experts),
        out_shape=(
            jax.ShapeDtypeStruct((rows, width + LANES), jnp.bfloat16),
            jax.ShapeDtypeStruct((rows, LANES), jnp.int32),
        ),
        compiler_params=pltpu.CompilerParams(vmem_limit_bytes=VMEM_BYTES),
        name="prepare",
    )(states, routes, jnp.asarray(order, jnp.bfloat16))


def pick_kernel(*refs, parts):
    sources, codes_refs = refs[:parts], refs[parts : 2 * parts]
    group_ref, wanted_ref, keep_ref, send_ref, onehot_ref = refs[2 * parts :]

    @pl.when(pl.program_id(0) == 0)
    def _():
        codes = jnp.concatenate([ref[...].astype(jnp.float32) for ref in codes_refs], axis=0).T
        wanted, group = wanted_ref[:, :1], group_ref[...]
        hits = jnp.zeros((wanted.shape[0], group.shape[1]), jnp.float32)
        for choice in range(TOPK):
            hits = jnp.where(codes[choice : choice + 1] + group == wanted, 1.0, hits)
        onehot_ref[...] = hits.astype(jnp.bfloat16)

    rows = jnp.concatenate([ref[...] for ref in sources], axis=0)
    kept = keep_ref.shape[0]
    picked = jnp.dot(onehot_ref[...], rows, preferred_element_type=jnp.float32)
    picked = picked.astype(keep_ref.dtype)
    keep_ref[...] = picked[:kept]
    send_ref[...] = picked[kept:]


def pick(sources, group, wanted, width):
    rows, slots = group.shape[1], wanted.shape[0]
    cuts = 2 if width % (2 * LANES) == 0 else 1
    block = width // cuts
    piece = lambda a: pl.BlockSpec((a.shape[0], block), lambda i: (0, i))
    codes = lambda a: pl.BlockSpec((a.shape[0], LANES), lambda i: (0, width // LANES))
    whole = lambda a: pl.BlockSpec(a.shape, lambda i: (0, 0))
    return pl.pallas_call(
        functools.partial(pick_kernel, parts=len(sources)),
        grid=(cuts,),
        in_specs=[piece(a) for a in sources]
        + [codes(a) for a in sources]
        + [whole(group), whole(wanted)],
        out_specs=[pl.BlockSpec((slots // 2, block), lambda i: (0, i))] * 2,
        out_shape=[jax.ShapeDtypeStruct((slots // 2, width), jnp.bfloat16)] * 2,
        scratch_shapes=[pltpu.VMEM((slots, rows), jnp.bfloat16)],
        compiler_params=pltpu.CompilerParams(vmem_limit_bytes=VMEM_BYTES),
        name="pick",
    )(*sources, *sources, group, wanted)


def expert_kernel(*refs, pairs, kept, sent, experts_local):
    x_refs, (place_ref, gate_ref, up_ref, out_ref, rows_ref) = refs[: 2 * pairs], refs[2 * pairs :]
    expert = pl.program_id(1)

    @pl.when(pl.program_id(0) == 0)
    def _():
        at = 0
        for number, x_ref in enumerate(x_refs):
            part = sent if number % 2 else kept
            rows_ref[expert, at : at + part, :] = x_ref[
                pl.ds(pl.multiple_of(expert * part, 16), part), :
            ]
            at += part

    rows = rows_ref[expert]
    gate = jnp.dot(rows, gate_ref[0], preferred_element_type=jnp.float32)
    up = jnp.dot(rows, up_ref[0], preferred_element_type=jnp.float32)
    inner = (gate / (1.0 + jnp.exp(-gate)) * up).astype(jnp.bfloat16)
    wanted = place_ref[...]
    base = expert * rows.shape[0]
    row_ids = lax.broadcasted_iota(jnp.int32, (wanted.shape[0], rows.shape[0]), 1) + base
    marks = (wanted == row_ids).astype(jnp.float32).astype(jnp.bfloat16)
    placed = jnp.dot(marks, inner, preferred_element_type=jnp.float32).astype(out_ref.dtype)

    @pl.when(expert == 0)
    def _():
        out_ref[...] = placed

    @pl.when(expert != 0)
    def _():
        out_ref[...] += placed


def run_experts(arrays, places, w_gate, w_up):
    experts_local, width, hidden = w_gate.shape
    kept, sent = arrays[0].shape[0] // experts_local, arrays[1].shape[0] // experts_local
    pairs = len(arrays) // 2
    rows = pairs * (kept + sent)
    block = 2 * LANES
    slots = places.shape[0]
    return pl.pallas_call(
        functools.partial(
            expert_kernel, pairs=pairs, kept=kept, sent=sent, experts_local=experts_local
        ),
        grid=(hidden // block, experts_local),
        in_specs=[pl.BlockSpec(a.shape, lambda f, e: (0, 0)) for a in arrays]
        + [pl.BlockSpec(places.shape, lambda f, e: (0, 0))]
        + [pl.BlockSpec((1, width, block), lambda f, e: (e, 0, f))] * 2,
        out_specs=pl.BlockSpec((slots, block), lambda f, e: (0, f)),
        out_shape=jax.ShapeDtypeStruct((slots, hidden), jnp.bfloat16),
        scratch_shapes=[pltpu.VMEM((experts_local, rows, width), jnp.bfloat16)],
        compiler_params=pltpu.CompilerParams(vmem_limit_bytes=VMEM_BYTES),
        name="experts",
    )(*arrays, places, w_gate, w_up)


def combine_kernel(back_ref, columns_ref, gates_ref, out_ref):
    tokens, steps, _ = out_ref.shape
    rows = tokens * steps
    slots, hidden = back_ref.shape
    gates = gates_ref[...]
    mixing = gates / jnp.sum(gates, axis=-1, keepdims=True)
    ids = lax.broadcasted_iota(jnp.int32, (rows, slots), 1)
    marks = [
        (columns_ref[:, choice : choice + 1] == ids).astype(jnp.float32) for choice in range(TOPK)
    ]
    picked = jnp.dot(
        jnp.concatenate(marks, axis=0).astype(jnp.bfloat16),
        back_ref[...],
        preferred_element_type=jnp.float32,
    )
    for choice in range(TOPK):
        scaled = picked[choice * rows : (choice + 1) * rows] * mixing[:, choice : choice + 1]
        scaled = scaled.astype(out_ref.dtype)
        for token in range(tokens):
            out_ref[token, :, choice * hidden : (choice + 1) * hidden] = scaled[
                token * steps : (token + 1) * steps
            ]


def combine(back, columns, gates, tokens, steps):
    return pl.pallas_call(
        combine_kernel,
        out_shape=jax.ShapeDtypeStruct((tokens, steps, TOPK * back.shape[1]), jnp.bfloat16),
        compiler_params=pltpu.CompilerParams(vmem_limit_bytes=12 * 1024 * 1024),
        name="combine",
    )(back, columns, gates)


def per_device(
    hidden_states,
    routes,
    gates,
    w_gate,
    w_up,
    queries,
    new_keys,
    new_values,
    cache_keys,
    cache_values,
    lengths,
):
    peers = lax.axis_size("expert")
    me = lax.axis_index("expert")
    lines = peers // INNER
    experts_local = w_gate.shape[0]
    experts = experts_local * peers
    steps_total, local_rows, model_width = hidden_states.shape
    capacity = local_rows * TOPK * 2 // experts
    slot_span = steps_total * capacity
    gate_full, up_full = (
        lax.all_gather(w_gate, "replica", axis=1, tiled=True),
        lax.all_gather(w_up, "replica", axis=1, tiled=True),
    )
    hidden_width = gate_full.shape[2]
    block_rows = steps_total * local_rows

    assert experts * capacity <= 256
    send = lambda array, target: lax.ppermute(array, "expert", moves(peers, target))
    to_line = lambda offset: lambda z, y, x, c: (z ^ offset, y, x, c)
    to_column = lambda z, y, x, c: (z, y, 1 - x, c)
    to_row = lambda z, y, x, c: (z, 1 - y, x, c)
    other_side = lambda z, y, x, c: (z, y, x, 1 - c)
    after = lambda array, *others: lax.optimization_barrier((array,) + others)[0]
    z, y, x, side = place(me)

    by_token = lambda a: jnp.swapaxes(a, 0, 1)
    payload, columns = prepare(
        by_token(hidden_states),
        by_token(routes).reshape(block_rows, TOPK),
        capacity,
        experts,
    )
    token = np.arange(4 * block_rows)
    group = (token // block_rows * steps_total + token % steps_total) * 256
    group = jnp.asarray(group, jnp.float32)[None]
    slots = np.arange(2 * experts_local * 4 * slot_span).reshape(
        2, experts_local, 4, steps_total, capacity
    )
    of_side, of_expert, of_block, of_step, of_slot = [
        number.reshape(-1) for number in np.indices(slots.shape)
    ]
    wanted_expert = jnp.where(of_side == 0, me, me ^ 1) * experts_local + of_expert
    wanted = wanted_expert * capacity + of_slot + (of_block * steps_total + of_step) * 256
    wanted = jnp.broadcast_to(wanted.astype(jnp.float32)[:, None], (slots.size, LANES))

    arrived = {0: payload}
    for offset in sorted(range(1, lines), key=lambda n: (n != 2, n)):
        source = after(payload, arrived[2]) if offset > 2 else payload
        arrived[offset] = send(source, to_line(offset))
    kept = 4 * slot_span
    numbers = jnp.arange(experts * slot_span, dtype=jnp.int32)
    owner, expert, rest = (
        numbers // (experts_local * slot_span),
        numbers // slot_span % experts_local,
        numbers % slot_span,
    )
    oz, oy, ox, oc = place(owner)
    within = jnp.where(oc == side, 0, kept) + ((oy ^ y) * 2 + (ox ^ x)) * slot_span + rest
    places = (expert * lines + (oz ^ z)) * 2 * kept + within

    blocks, cut = [], padded(block_rows // 2)
    hops, fars, keeps = [], [], []
    for offset in range(lines):
        own = arrived[offset]
        if offset == 1:
            own = after(own, *fars[0], places)
        elif offset > 2:
            own = after(own, *hops[offset - 2], keeps[0])
        column, row = send(own, to_column), send(own, to_row)
        hops.append((column, row))
        far = send(column[:cut], to_row), send(row[cut:], to_column)
        fars.append(far)
        keep, give = pick([own, column, row, *far], group, wanted, model_width)
        keeps.append(keep)
        blocks += [keep, send(give, other_side)]

    outgoing = run_experts(blocks, places[:, None], gate_full, up_full)
    outgoing = outgoing.reshape(peers, experts_local * slot_span, hidden_width)
    returned = lax.all_to_all(outgoing, "expert", split_axis=0, concat_axis=0, tiled=True)
    attn_out = attention(
        queries, new_keys, new_values, cache_keys, cache_values, after(lengths, outgoing)
    )
    back_rows = returned.reshape(experts * slot_span, hidden_width)
    moe_hidden = combine(
        back_rows, columns, by_token(gates).reshape(block_rows, TOPK), local_rows, steps_total
    )
    return (by_token(moe_hidden), attn_out)


def solution(mesh):
    in_specs = (
        P(None, ("replica", "expert"), None),
        P(None, ("replica", "expert"), None),
        P(None, ("replica", "expert"), None),
        P("expert", "replica", None),
        P("expert", "replica", None),
        P(None, ("replica", "expert"), None),
        P(None, ("replica", "expert"), None),
        P(None, ("replica", "expert"), None),
        P(("replica", "expert"), None, None),
        P(("replica", "expert"), None, None),
        P(("replica", "expert")),
    )
    out_specs = (P(None, ("replica", "expert"), None), P(None, ("replica", "expert"), None))
    return jax.shard_map(
        per_device, mesh=mesh, in_specs=in_specs, out_specs=out_specs, check_vma=False
    )
```

```python
import functools
import math

import jax
import jax.numpy as jnp
import numpy as np
from jax import lax
from jax.experimental import pallas as pl
from jax.experimental.pallas import tpu as pltpu
from jax.sharding import PartitionSpec as P

HQ = 64
KVH = 4
HD = 128
TOPK = 8
LANES = 128
EDGE = 2
INNER = EDGE**3
VMEM_BYTES = 50 * 1024 * 1024
EXPERT_VMEM = 50 * 1024 * 1024


def attention_kernel(lengths_ref, q_ref, nk_ref, nv_ref, k_ref, v_ref, out_ref, *, groups):
    rows, steps, _ = q_ref.shape
    cache = k_ref.shape[1]
    extra = 16
    many = steps*groups
    scale = 1.0/math.sqrt(HD)
    shape = (cache+extra, 2*many)
    position = lax.broadcasted_iota(jnp.int32, shape, 0)
    step = lax.broadcasted_iota(jnp.int32, shape, 1) % steps
    first = pl.program_id(0)*rows
    pad = jnp.zeros((extra-steps, 2*HD), jnp.float32)
    none = jnp.zeros((many, HD), jnp.float32)
    for r in range(rows):
        limit = jnp.where(position < cache, lengths_ref[first + r], step + (cache + 1))
        valid = position < limit
        for pair in range(KVH//2):
            wide = pl.ds(pair*2*HD, 2*HD)
            def with_new(cached, new):
                fresh = jnp.concatenate([new[r, :, wide].astype(jnp.float32), pad], axis=0)
                return jnp.concatenate([cached[r, :, wide], fresh.astype(jnp.bfloat16)], axis=0)
            heads = [q_ref[r, :, (pair*2*groups+h)*HD:(pair*2*groups+h+1)*HD].astype(jnp.float32) for h in range(2*groups)]
            low = jnp.concatenate(heads[:groups], axis=0)
            high = jnp.concatenate(heads[groups:], axis=0)
            asked = jnp.concatenate([jnp.concatenate([low, none], axis=1), jnp.concatenate([none, high], axis=1)], axis=0).astype(jnp.bfloat16)
            scores = lax.dot_general(with_new(k_ref, nk_ref), asked, (((1,),(1,)),((),())), preferred_element_type=jnp.float32)*scale
            scores = jnp.where(valid, scores, -jnp.inf)
            weights = jnp.exp(scores - jnp.max(scores, axis=0, keepdims=True))
            probs = (weights * (1.0/jnp.sum(weights, axis=0, keepdims=True))).astype(jnp.bfloat16)
            mixed = lax.dot_general(probs, with_new(v_ref, nv_ref), (((0,),(0,)),((),())), preferred_element_type=jnp.float32)
            for h in range(2*groups):
                at = h//groups*HD
                out_ref[r, :, (pair*2*groups+h)*HD:(pair*2*groups+h+1)*HD] = mixed[h*steps:(h+1)*steps, at:at+HD].astype(out_ref.dtype)

def attention(queries,new_keys,new_values,cache_keys,cache_values,lengths):
    steps, rows, _ = queries.shape
    groups = HQ//KVH
    cache = cache_keys.shape[1]
    part = max(n for n in range(1,8) if rows % n == 0)
    turn = lambda a: jnp.swapaxes(a,0,1)
    spec = lambda a: pl.BlockSpec((part,)+a.shape[1:], lambda i:(i,0,0))
    arrays = (turn(queries), turn(new_keys), turn(new_values), cache_keys, cache_values)
    out= pl.pallas_call(
        functools.partial(attention_kernel, groups=groups),
        grid=(rows//part,),
        in_specs=[pl.BlockSpec(memory_space=pltpu.SMEM)]+[spec(a) for a in arrays],
        out_specs=spec(arrays[0]),
        out_shape=jax.ShapeDtypeStruct(arrays[0].shape, queries.dtype),
        compiler_params=pltpu.CompilerParams(vmem_limit_bytes=16 * 1024 * 1024),
        name="attention",
    )(lengths, *arrays)
    return turn(out)


def place(index):
    return index // INNER, index // 4 % EDGE, index // 2 % EDGE, index % EDGE


def device_at(line, row, column, side):
    return ((line * EDGE + row) * EDGE + column) * EDGE + side


def moves(peers, target):
    pairs = [(index, target(*place(index))) for index in range(peers)]
    return [(index, device_at(*to)) for index, to in pairs if to is not None]


def padded(rows):
    return -(-rows // 16) * 16


def prepare_kernel(states_ref, routes_ref, payload_ref, columns_ref, *, capacity, experts):
    tokens, steps, width = states_ref.shape
    states = jnp.concatenate(
        [states_ref[token].astype(jnp.float32) for token in range(tokens)], axis=0
    )
    scale = lax.rsqrt(jnp.mean(states * states, axis=-1, keepdims=True) + 1e-06)
    payload_ref[:, :width] = (states * scale).astype(payload_ref.dtype)
    rows = tokens * steps
    row_ids = lax.broadcasted_iota(jnp.int32, (rows, tokens), 0)
    row_tokens = row_ids // steps == lax.broadcasted_iota(jnp.int32, (rows, tokens), 1)
    routes = sum(
        lax.dot_general(
            (row_tokens & (row_ids % steps == step)).astype(jnp.float32).astype(jnp.bfloat16),
            routes_ref[step].astype(jnp.float32).astype(jnp.bfloat16),
            (((1,), (1,)), ((), ())),
            preferred_element_type=jnp.float32,
        )
        for step in range(steps)
    ).astype(jnp.int32)
    first = lax.broadcasted_iota(jnp.int32, (rows, rows), 0)
    second = lax.broadcasted_iota(jnp.int32, (rows, rows), 1)
    order = ((first % steps == second % steps) & (first > second)).astype(jnp.float32)
    expert_ids = lax.broadcasted_iota(jnp.int32, (rows, experts), 1)
    marks = [
        (routes[:, choice : choice + 1] == expert_ids).astype(jnp.float32)
        for choice in range(TOPK)
    ]
    named = sum(marks)
    earlier = jnp.dot(
        order.astype(jnp.bfloat16), named.astype(jnp.bfloat16), preferred_element_type=jnp.float32
    )
    lane_ids = lax.broadcasted_iota(jnp.int32, (rows, LANES), 1)
    step = lax.broadcasted_iota(jnp.int32, (rows, 1), 0) % steps
    codes = jnp.zeros((rows, LANES), jnp.float32)
    columns = jnp.zeros((rows, LANES), jnp.int32)
    for choice in range(TOPK):
        slot = jnp.sum(earlier * marks[choice], axis=-1, keepdims=True)
        expert = routes[:, choice : choice + 1]
        code = expert.astype(jnp.float32) * capacity + slot
        codes = jnp.where(lane_ids == choice, code, codes)
        column = (expert * steps + step) * capacity + slot.astype(jnp.int32)
        columns = jnp.where(lane_ids == choice, column, columns)
    payload_ref[:, width:] = codes.astype(payload_ref.dtype)
    columns_ref[...] = columns


def prepare(states, routes, capacity, experts):
    tokens, steps, width = states.shape
    rows = tokens * steps
    return pl.pallas_call(
        functools.partial(prepare_kernel, capacity=capacity, experts=experts),
        out_shape=(
            jax.ShapeDtypeStruct((rows, width + LANES), jnp.bfloat16),
            jax.ShapeDtypeStruct((rows, LANES), jnp.int32),
        ),
        compiler_params=pltpu.CompilerParams(vmem_limit_bytes=VMEM_BYTES),
        name="prepare",
    )(states, routes)


def pick_kernel(*refs, parts):
    sources, codes_refs = refs[:parts], refs[parts : 2 * parts]
    group_ref, wanted_ref, keep_ref, send_ref, onehot_ref = refs[2 * parts :]

    @pl.when(pl.program_id(0) == 0)
    def _():
        codes = jnp.concatenate([ref[...].astype(jnp.float32) for ref in codes_refs], axis=0).T
        wanted, group = wanted_ref[:, :1], group_ref[...]
        hits = jnp.zeros((wanted.shape[0], group.shape[1]), jnp.float32)
        for choice in range(TOPK):
            hits = jnp.where(codes[choice : choice + 1] + group == wanted, 1.0, hits)
        onehot_ref[...] = hits.astype(jnp.bfloat16)

    rows = jnp.concatenate([ref[...] for ref in sources], axis=0)
    kept = keep_ref.shape[0]
    picked = jnp.dot(onehot_ref[...], rows, preferred_element_type=jnp.float32)
    picked = picked.astype(keep_ref.dtype)
    keep_ref[...] = picked[:kept]
    send_ref[...] = picked[kept:]


def pick(sources, group, wanted, width):
    rows, slots = group.shape[1], wanted.shape[0]
    cuts = 2 if width % (2 * LANES) == 0 else 1
    block = width // cuts
    sources = [source if isinstance(source, tuple) else (source, 0, 1) for source in sources]
    arrays = [source[0] for source in sources]
    piece = lambda a, n, of: pl.BlockSpec((a.shape[0] // of, block), lambda i: (n, i))
    codes = lambda a, n, of: pl.BlockSpec((a.shape[0] // of, LANES), lambda i: (n, width // LANES))
    whole = lambda a: pl.BlockSpec(a.shape, lambda i: (0, 0))
    return pl.pallas_call(
        functools.partial(pick_kernel, parts=len(sources)),
        grid=(cuts,),
        in_specs=[piece(*source) for source in sources]
        + [codes(*source) for source in sources]
        + [whole(group), whole(wanted)],
        out_specs=[pl.BlockSpec((slots // 2, block), lambda i: (0, i))] * 2,
        out_shape=[jax.ShapeDtypeStruct((slots // 2, width), jnp.bfloat16)] * 2,
        scratch_shapes=[pltpu.VMEM((slots, rows), jnp.bfloat16)],
        compiler_params=pltpu.CompilerParams(vmem_limit_bytes=VMEM_BYTES),
        name="pick",
    )(*arrays, *arrays, group, wanted)


def expert_kernel(owners_ref, *refs, count, part):
    x_refs, (gate_ref, up_ref, out_ref, rows_ref, arrived) = refs[:count], refs[count:]
    hidden_part, expert = pl.program_id(0), pl.program_id(1)
    experts_local = rows_ref.shape[0]
    span = out_ref.shape[1] // experts_local

    def copy(number, which):
        return pltpu.make_async_copy(
            x_refs[number].at[pl.ds(which * part, part)],
            rows_ref.at[which, pl.ds(number * part, part)],
            arrived.at[which, number],
        )

    @pl.when((hidden_part == 0) & (expert == 0))
    def _():
        for which in range(experts_local):
            for number in range(count):
                copy(number, which).start()

    for which in range(experts_local):

        @pl.when((hidden_part == 0) & (expert == which))
        def _():
            for number in range(count):
                copy(number, which).wait()

    rows = rows_ref[expert]
    gate = jnp.dot(rows, gate_ref[0], preferred_element_type=jnp.float32)
    up = jnp.dot(rows, up_ref[0], preferred_element_type=jnp.float32)
    inner = (gate / (1.0 + jnp.exp(-gate)) * up).astype(out_ref.dtype)
    for which in range(experts_local):

        @pl.when(expert == which)
        def _():
            for group in range(owners_ref.shape[0]):
                out_ref[owners_ref[group], which * span : (which + 1) * span, :] = inner[
                    group * span : (group + 1) * span
                ]


def run_experts(arrays, owners, span, w_gate, w_up):
    experts_local, width, hidden = w_gate.shape
    part, count = arrays[0].shape[0] // experts_local, len(arrays)
    rows = count * part
    block = 2 * LANES
    return pl.pallas_call(
        functools.partial(expert_kernel, count=count, part=part),
        grid=(hidden // block, experts_local),
        in_specs=[pl.BlockSpec(memory_space=pltpu.SMEM)]
        + [pl.BlockSpec(memory_space=pl.ANY)] * count
        + [pl.BlockSpec((1, width, block), lambda f, e: (e, 0, f))] * 2,
        out_specs=pl.BlockSpec(
            (owners.shape[0], experts_local * span, block), lambda f, e: (0, 0, f)
        ),
        out_shape=jax.ShapeDtypeStruct(
            (owners.shape[0], experts_local * span, hidden), jnp.bfloat16
        ),
        scratch_shapes=[
            pltpu.VMEM((experts_local, rows, width), jnp.bfloat16),
            pltpu.SemaphoreType.DMA((experts_local, count)),
        ],
        compiler_params=pltpu.CompilerParams(vmem_limit_bytes=EXPERT_VMEM),
        name="experts",
    )(owners, *arrays, w_gate, w_up)


def combine_kernel(back_ref, columns_ref, gates_ref, out_ref):
    tokens, steps, _ = out_ref.shape
    rows = tokens * steps
    slots, hidden = back_ref.shape
    gates = gates_ref[...]
    mixing = gates / jnp.sum(gates, axis=-1, keepdims=True)
    ids = lax.broadcasted_iota(jnp.int32, (rows, slots), 1)
    marks = [
        (columns_ref[:, choice : choice + 1] == ids).astype(jnp.float32) for choice in range(TOPK)
    ]
    picked = jnp.dot(
        jnp.concatenate(marks, axis=0).astype(jnp.bfloat16),
        back_ref[...],
        preferred_element_type=jnp.float32,
    )
    for choice in range(TOPK):
        scaled = picked[choice * rows : (choice + 1) * rows] * mixing[:, choice : choice + 1]
        scaled = scaled.astype(out_ref.dtype)
        for token in range(tokens):
            out_ref[token, :, choice * hidden : (choice + 1) * hidden] = scaled[
                token * steps : (token + 1) * steps
            ]


def combine(back, columns, gates, tokens, steps):
    return pl.pallas_call(
        combine_kernel,
        out_shape=jax.ShapeDtypeStruct((tokens, steps, TOPK * back.shape[1]), jnp.bfloat16),
        compiler_params=pltpu.CompilerParams(vmem_limit_bytes=12 * 1024 * 1024),
        name="combine",
    )(back, columns, gates)


def per_device(
    hidden_states,
    routes,
    gates,
    w_gate,
    w_up,
    queries,
    new_keys,
    new_values,
    cache_keys,
    cache_values,
    lengths,
):
    peers = lax.axis_size("expert")
    me = lax.axis_index("expert")
    lines = peers // INNER
    experts_local = w_gate.shape[0]
    experts = experts_local * peers
    steps_total, local_rows, model_width = hidden_states.shape
    capacity = local_rows * TOPK * 2 // experts
    slot_span = steps_total * capacity
    gate_full, up_full = (
        lax.all_gather(w_gate, "replica", axis=1, tiled=True),
        lax.all_gather(w_up, "replica", axis=1, tiled=True),
    )
    hidden_width = gate_full.shape[2]
    block_rows = steps_total * local_rows

    assert experts * capacity <= 256
    send = lambda array, target: lax.ppermute(array, "expert", moves(peers, target))
    to_line = lambda offset: lambda z, y, x, c: (z ^ offset, y, x, c)
    to_column = lambda z, y, x, c: (z, y, 1 - x, c)
    to_row = lambda z, y, x, c: (z, 1 - y, x, c)
    other_side = lambda z, y, x, c: (z, y, x, 1 - c)
    after = lambda array, *others: lax.optimization_barrier((array,) + others)[0]

    by_token = lambda a: jnp.swapaxes(a, 0, 1)
    payload, columns = prepare(
        by_token(hidden_states),
        jnp.swapaxes(routes, 1, 2),
        capacity,
        experts,
    )
    me = after(me, columns)
    z, y, x, side = place(me)
    token = np.arange(4 * block_rows)
    group = (token // block_rows * steps_total + token % steps_total) * 256
    group = jnp.asarray(group, jnp.float32)[None]
    slots = np.arange(2 * experts_local * 4 * slot_span).reshape(
        2, experts_local, 4, steps_total, capacity
    )
    of_side, of_expert, of_block, of_step, of_slot = [
        number.reshape(-1) for number in np.indices(slots.shape)
    ]
    wanted_expert = jnp.where(of_side == 0, me, me ^ 1) * experts_local + of_expert
    wanted = wanted_expert * capacity + of_slot + (of_block * steps_total + of_step) * 256
    wanted = jnp.broadcast_to(wanted.astype(jnp.float32)[:, None], (slots.size, LANES))

    planes = [z ^ offset for offset in range(lines)]
    if lines == 4:
        inner, beyond = (z == 1) | (z == 2), z // 2 * 2 ^ 2
        planes[2:] = [beyond + z // 2, beyond + 1 - z // 2]
    group_id = np.arange(peers)
    owners = device_at(
        jnp.stack(planes)[group_id // INNER],
        y ^ group_id // 2 % EDGE,
        x ^ group_id % EDGE,
        side ^ group_id // 4 % EDGE,
    ).astype(jnp.int32)

    blocks, keeps, cut = [], [], padded(block_rows // 2)

    def add_item(sources):
        keep, give = pick(sources, group, wanted, model_width)
        keeps.append(keep)
        blocks.extend([keep, send(give, other_side)])

    column, row = send(payload, to_column), send(payload, to_row)
    if lines == 4:
        middle = lambda z, y, x, c: (3 - z, y, x, c) if z in (1, 2) else None
        outward = lambda z, y, x, c: (z ^ 1, y, x, c) if z in (1, 2) else None
        next_line = send(payload, to_line(1))
        near_plane = send(after(payload, wanted), middle)
        far_plane = send(next_line, middle)
        near_out = send(near_plane, outward)
        far_out = send(far_plane, outward)
        halves = column[:cut], row[cut:]
        far = send(halves[0], to_row), send(halves[1], to_column)
        add_item([after(payload, far_plane), column, row, *far])
        own = after(next_line, *halves, owners)
        column, row = send(own, to_column), send(own, to_row)
        halves = column, row
        far = send(far[0], to_line(1)), send(far[1], to_line(1))
        add_item([own, column, row, *far])
        own = after(jnp.where(inner, near_plane, near_out), *halves)
        column, row = send(own, to_column), send(own, to_row)
        halves = column[:cut], row[cut:]
        past, far = far, (send(halves[0], to_row), send(halves[1], to_column))
        add_item([own, column, row, *far])
        own = after(jnp.where(inner, far_plane, far_out), *halves, *past, keeps[0])
        column, row = send(own, to_column), send(own, to_row)
        halves = lax.optimization_barrier((column[:cut], row[cut:], *far, keeps[1]))[:2]
        far = send(halves[0], to_row), send(halves[1], to_column)
        add_item([own, column, row, *far])
    else:
        for offset in range(lines):
            own = send(payload, to_line(offset)) if offset else payload
            if offset:
                column, row = send(own, to_column), send(own, to_row)
            far = send(column[:cut], to_row), send(row[cut:], to_column)
            add_item([own, column, row, *far])
    outgoing = run_experts(blocks, owners, slot_span, gate_full, up_full)
    returned = lax.all_to_all(outgoing, "expert", split_axis=0, concat_axis=0, tiled=True)
    attn_out = attention(
        queries, new_keys, new_values, cache_keys, cache_values, after(lengths, outgoing)
    )
    back_rows = returned.reshape(experts * slot_span, hidden_width)
    moe_hidden = combine(
        back_rows, columns, by_token(gates).reshape(block_rows, TOPK), local_rows, steps_total
    )
    return (by_token(moe_hidden), attn_out)


def solution(mesh):
    in_specs = (
        P(None, ("replica", "expert"), None),
        P(None, ("replica", "expert"), None),
        P(None, ("replica", "expert"), None),
        P("expert", "replica", None),
        P("expert", "replica", None),
        P(None, ("replica", "expert"), None),
        P(None, ("replica", "expert"), None),
        P(None, ("replica", "expert"), None),
        P(("replica", "expert"), None, None),
        P(("replica", "expert"), None, None),
        P(("replica", "expert")),
    )
    out_specs = (P(None, ("replica", "expert"), None), P(None, ("replica", "expert"), None))
    return jax.shard_map(
        per_device, mesh=mesh, in_specs=in_specs, out_specs=out_specs, check_vma=False
    )
```

```python
import functools
import math

import jax
import jax.numpy as jnp
import numpy as np
from jax import lax
from jax.experimental import pallas as pl
from jax.experimental.pallas import tpu as pltpu
from jax.sharding import PartitionSpec as P

HQ = 64
KVH = 4
HD = 128
TOPK = 8
LANES = 128
EDGE = 2
INNER = EDGE**3
VMEM_BYTES = 50 * 1024 * 1024
EXPERT_VMEM = 50 * 1024 * 1024


def attention_kernel(lengths_ref, q_ref, nk_ref, nv_ref, k_ref, v_ref, out_ref, *, groups):
    rows, steps, _ = q_ref.shape
    cache = k_ref.shape[1]
    extra = 16
    many = steps*groups
    scale = 1.0/math.sqrt(HD)
    shape = (cache+extra, 2*many)
    position = lax.broadcasted_iota(jnp.int32, shape, 0)
    step = lax.broadcasted_iota(jnp.int32, shape, 1) % steps
    first = pl.program_id(0)*rows
    pad = jnp.zeros((extra-steps, 2*HD), jnp.float32)
    none = jnp.zeros((many, HD), jnp.float32)
    for r in range(rows):
        limit = jnp.where(position < cache, lengths_ref[first + r], step + (cache + 1))
        valid = position < limit
        for pair in range(KVH//2):
            wide = pl.ds(pair*2*HD, 2*HD)
            def with_new(cached, new):
                fresh = jnp.concatenate([new[r, :, wide].astype(jnp.float32), pad], axis=0)
                return jnp.concatenate([cached[r, :, wide], fresh.astype(jnp.bfloat16)], axis=0)
            heads = [q_ref[r, :, (pair*2*groups+h)*HD:(pair*2*groups+h+1)*HD].astype(jnp.float32) for h in range(2*groups)]
            low = jnp.concatenate(heads[:groups], axis=0)
            high = jnp.concatenate(heads[groups:], axis=0)
            asked = jnp.concatenate([jnp.concatenate([low, none], axis=1), jnp.concatenate([none, high], axis=1)], axis=0).astype(jnp.bfloat16)
            scores = lax.dot_general(with_new(k_ref, nk_ref), asked, (((1,),(1,)),((),())), preferred_element_type=jnp.float32)*scale
            scores = jnp.where(valid, scores, -jnp.inf)
            weights = jnp.exp(scores - jnp.max(scores, axis=0, keepdims=True))
            probs = (weights * (1.0/jnp.sum(weights, axis=0, keepdims=True))).astype(jnp.bfloat16)
            mixed = lax.dot_general(probs, with_new(v_ref, nv_ref), (((0,),(0,)),((),())), preferred_element_type=jnp.float32)
            for h in range(2*groups):
                at = h//groups*HD
                out_ref[r, :, (pair*2*groups+h)*HD:(pair*2*groups+h+1)*HD] = mixed[h*steps:(h+1)*steps, at:at+HD].astype(out_ref.dtype)

def attention(queries,new_keys,new_values,cache_keys,cache_values,lengths):
    steps, rows, _ = queries.shape
    groups = HQ//KVH
    cache = cache_keys.shape[1]
    part = max(n for n in range(1,8) if rows % n == 0)
    turn = lambda a: jnp.swapaxes(a,0,1)
    spec = lambda a: pl.BlockSpec((part,)+a.shape[1:], lambda i:(i,0,0))
    arrays = (turn(queries), turn(new_keys), turn(new_values), cache_keys, cache_values)
    out= pl.pallas_call(
        functools.partial(attention_kernel, groups=groups),
        grid=(rows//part,),
        in_specs=[pl.BlockSpec(memory_space=pltpu.SMEM)]+[spec(a) for a in arrays],
        out_specs=spec(arrays[0]),
        out_shape=jax.ShapeDtypeStruct(arrays[0].shape, queries.dtype),
        compiler_params=pltpu.CompilerParams(vmem_limit_bytes=16 * 1024 * 1024),
        name="attention",
    )(lengths, *arrays)
    return turn(out)


def place(index):
    return index // INNER, index // 4 % EDGE, index // 2 % EDGE, index % EDGE


def device_at(line, row, column, side):
    return ((line * EDGE + row) * EDGE + column) * EDGE + side


def moves(peers, target):
    pairs = [(index, target(*place(index))) for index in range(peers)]
    return [(index, device_at(*to)) for index, to in pairs if to is not None]


def padded(rows):
    return -(-rows // 16) * 16


def prepare_kernel(states_ref, routes_ref, payload_ref, columns_ref, *, capacity, experts):
    tokens, steps, width = states_ref.shape
    states = jnp.concatenate(
        [states_ref[token].astype(jnp.float32) for token in range(tokens)], axis=0
    )
    scale = lax.rsqrt(jnp.mean(states * states, axis=-1, keepdims=True) + 1e-06)
    payload_ref[:, :width] = (states * scale).astype(payload_ref.dtype)
    rows = tokens * steps
    row_ids = lax.broadcasted_iota(jnp.int32, (rows, tokens), 0)
    row_tokens = row_ids // steps == lax.broadcasted_iota(jnp.int32, (rows, tokens), 1)
    routes = sum(
        lax.dot_general(
            (row_tokens & (row_ids % steps == step)).astype(jnp.float32).astype(jnp.bfloat16),
            routes_ref[step].astype(jnp.float32).astype(jnp.bfloat16),
            (((1,), (1,)), ((), ())),
            preferred_element_type=jnp.float32,
        )
        for step in range(steps)
    ).astype(jnp.int32)
    first = lax.broadcasted_iota(jnp.int32, (rows, rows), 0)
    second = lax.broadcasted_iota(jnp.int32, (rows, rows), 1)
    order = ((first % steps == second % steps) & (first > second)).astype(jnp.float32)
    expert_ids = lax.broadcasted_iota(jnp.int32, (rows, experts), 1)
    marks = [
        (routes[:, choice : choice + 1] == expert_ids).astype(jnp.float32)
        for choice in range(TOPK)
    ]
    named = sum(marks)
    earlier = jnp.dot(
        order.astype(jnp.bfloat16), named.astype(jnp.bfloat16), preferred_element_type=jnp.float32
    )
    lane_ids = lax.broadcasted_iota(jnp.int32, (rows, LANES), 1)
    step = lax.broadcasted_iota(jnp.int32, (rows, 1), 0) % steps
    codes = jnp.zeros((rows, LANES), jnp.float32)
    columns = jnp.zeros((rows, LANES), jnp.int32)
    for choice in range(TOPK):
        slot = jnp.sum(earlier * marks[choice], axis=-1, keepdims=True)
        expert = routes[:, choice : choice + 1]
        code = expert.astype(jnp.float32) * capacity + slot
        codes = jnp.where(lane_ids == choice, code, codes)
        column = (expert * steps + step) * capacity + slot.astype(jnp.int32)
        columns = jnp.where(lane_ids == choice, column, columns)
    payload_ref[:, width:] = codes.astype(payload_ref.dtype)
    columns_ref[...] = columns


def prepare(states, routes, capacity, experts):
    tokens, steps, width = states.shape
    rows = tokens * steps
    return pl.pallas_call(
        functools.partial(prepare_kernel, capacity=capacity, experts=experts),
        out_shape=(
            jax.ShapeDtypeStruct((rows, width + LANES), jnp.bfloat16),
            jax.ShapeDtypeStruct((rows, LANES), jnp.int32),
        ),
        compiler_params=pltpu.CompilerParams(vmem_limit_bytes=VMEM_BYTES),
        name="prepare",
    )(states, routes)


def pick_kernel(*refs, parts):
    sources, codes_refs = refs[:parts], refs[parts : 2 * parts]
    group_ref, wanted_ref, keep_ref, send_ref, onehot_ref = refs[2 * parts :]

    @pl.when(pl.program_id(0) == 0)
    def _():
        codes = jnp.concatenate([ref[...].astype(jnp.float32) for ref in codes_refs], axis=0).T
        wanted, group = wanted_ref[:, :1], group_ref[...]
        hits = jnp.zeros((wanted.shape[0], group.shape[1]), jnp.float32)
        for choice in range(TOPK):
            hits = jnp.where(codes[choice : choice + 1] + group == wanted, 1.0, hits)
        onehot_ref[...] = hits.astype(jnp.bfloat16)

    rows = jnp.concatenate([ref[...] for ref in sources], axis=0)
    kept = keep_ref.shape[0]
    picked = jnp.dot(onehot_ref[...], rows, preferred_element_type=jnp.float32)
    picked = picked.astype(keep_ref.dtype)
    keep_ref[...] = picked[:kept]
    send_ref[...] = picked[kept:]


def pick(sources, group, wanted, width):
    rows, slots = group.shape[1], wanted.shape[0]
    cuts = 2 if width % (2 * LANES) == 0 else 1
    block = width // cuts
    sources = [source if isinstance(source, tuple) else (source, 0, 1) for source in sources]
    arrays = [source[0] for source in sources]
    piece = lambda a, n, of: pl.BlockSpec((a.shape[0] // of, block), lambda i: (n, i))
    codes = lambda a, n, of: pl.BlockSpec((a.shape[0] // of, LANES), lambda i: (n, width // LANES))
    whole = lambda a: pl.BlockSpec(a.shape, lambda i: (0, 0))
    return pl.pallas_call(
        functools.partial(pick_kernel, parts=len(sources)),
        grid=(cuts,),
        in_specs=[piece(*source) for source in sources]
        + [codes(*source) for source in sources]
        + [whole(group), whole(wanted)],
        out_specs=[pl.BlockSpec((slots // 2, block), lambda i: (0, i))] * 2,
        out_shape=[jax.ShapeDtypeStruct((slots // 2, width), jnp.bfloat16)] * 2,
        scratch_shapes=[pltpu.VMEM((slots, rows), jnp.bfloat16)],
        compiler_params=pltpu.CompilerParams(vmem_limit_bytes=VMEM_BYTES),
        name="pick",
    )(*arrays, *arrays, group, wanted)


def expert_kernel(owners_ref, *refs, count, part, earlier):
    x_refs, refs = refs[:count], refs[count:]
    done_ref, refs = (refs[0], refs[1:]) if earlier else (None, refs)
    gate_ref, up_ref, out_ref, rows_ref, arrived = refs
    hidden_part, expert = pl.program_id(0), pl.program_id(1)
    experts_local = rows_ref.shape[0]
    span = out_ref.shape[1] // experts_local

    def copy(number, which):
        return pltpu.make_async_copy(
            x_refs[number].at[pl.ds(which * part, part)],
            rows_ref.at[which, pl.ds(number * part, part)],
            arrived.at[which, number],
        )

    @pl.when((hidden_part == 0) & (expert == 0))
    def _():
        for which in range(experts_local):
            for number in range(count):
                copy(number, which).start()

    for which in range(experts_local):

        @pl.when((hidden_part == 0) & (expert == which))
        def _():
            for number in range(count):
                copy(number, which).wait()

    if earlier:

        @pl.when(expert == 0)
        def _():
            first = owners_ref[owners_ref.shape[0] - 1]
            out_ref[pl.ds(first, done_ref.shape[0])] = done_ref[...]

    rows = rows_ref[expert]
    gate = jnp.dot(rows, gate_ref[0], preferred_element_type=jnp.float32)
    up = jnp.dot(rows, up_ref[0], preferred_element_type=jnp.float32)
    inner = (gate / (1.0 + jnp.exp(-gate)) * up).astype(out_ref.dtype)
    for which in range(experts_local):

        @pl.when(expert == which)
        def _():
            for group in range(rows_ref.shape[1] // span):
                out_ref[owners_ref[group], which * span : (which + 1) * span, :] = inner[
                    group * span : (group + 1) * span
                ]


def run_experts(arrays, owners, span, w_gate, w_up, earlier=None):
    experts_local, width, hidden = w_gate.shape
    part, count = arrays[0].shape[0] // experts_local, len(arrays)
    rows = count * part
    block = 2 * LANES
    done = [] if earlier is None else [earlier]
    places = rows // span + sum(a.shape[0] for a in done)
    return pl.pallas_call(
        functools.partial(
            expert_kernel, count=count, part=part, earlier=earlier is not None
        ),
        grid=(hidden // block, experts_local),
        in_specs=[pl.BlockSpec(memory_space=pltpu.SMEM)]
        + [pl.BlockSpec(memory_space=pl.ANY)] * count
        + [pl.BlockSpec(a.shape[:2] + (block,), lambda f, e: (0, 0, f)) for a in done]
        + [pl.BlockSpec((1, width, block), lambda f, e: (e, 0, f))] * 2,
        out_specs=pl.BlockSpec(
            (places, experts_local * span, block), lambda f, e: (0, 0, f)
        ),
        out_shape=jax.ShapeDtypeStruct(
            (places, experts_local * span, hidden), jnp.bfloat16
        ),
        scratch_shapes=[
            pltpu.VMEM((experts_local, rows, width), jnp.bfloat16),
            pltpu.SemaphoreType.DMA((experts_local, count)),
        ],
        compiler_params=pltpu.CompilerParams(vmem_limit_bytes=EXPERT_VMEM),
        name="experts",
    )(owners, *arrays, *done, w_gate, w_up)


def combine_kernel(back_ref, columns_ref, gates_ref, out_ref):
    tokens, steps, _ = out_ref.shape
    rows = tokens * steps
    slots, hidden = back_ref.shape
    gates = gates_ref[...]
    mixing = gates / jnp.sum(gates, axis=-1, keepdims=True)
    ids = lax.broadcasted_iota(jnp.int32, (rows, slots), 1)
    marks = [
        (columns_ref[:, choice : choice + 1] == ids).astype(jnp.float32) for choice in range(TOPK)
    ]
    picked = jnp.dot(
        jnp.concatenate(marks, axis=0).astype(jnp.bfloat16),
        back_ref[...],
        preferred_element_type=jnp.float32,
    )
    for choice in range(TOPK):
        scaled = picked[choice * rows : (choice + 1) * rows] * mixing[:, choice : choice + 1]
        scaled = scaled.astype(out_ref.dtype)
        for token in range(tokens):
            out_ref[token, :, choice * hidden : (choice + 1) * hidden] = scaled[
                token * steps : (token + 1) * steps
            ]


def combine(back, columns, gates, tokens, steps):
    return pl.pallas_call(
        combine_kernel,
        out_shape=jax.ShapeDtypeStruct((tokens, steps, TOPK * back.shape[1]), jnp.bfloat16),
        compiler_params=pltpu.CompilerParams(vmem_limit_bytes=12 * 1024 * 1024),
        name="combine",
    )(back, columns, gates)


def per_device(
    hidden_states,
    routes,
    gates,
    w_gate,
    w_up,
    queries,
    new_keys,
    new_values,
    cache_keys,
    cache_values,
    lengths,
):
    peers = lax.axis_size("expert")
    me = lax.axis_index("expert")
    lines = peers // INNER
    experts_local = w_gate.shape[0]
    experts = experts_local * peers
    steps_total, local_rows, model_width = hidden_states.shape
    capacity = local_rows * TOPK * 2 // experts
    slot_span = steps_total * capacity
    gate_full, up_full = (
        lax.all_gather(w_gate, "replica", axis=1, tiled=True),
        lax.all_gather(w_up, "replica", axis=1, tiled=True),
    )
    hidden_width = gate_full.shape[2]
    block_rows = steps_total * local_rows

    assert experts * capacity <= 256
    send = lambda array, target: lax.ppermute(array, "expert", moves(peers, target))
    to_line = lambda offset: lambda z, y, x, c: (z ^ offset, y, x, c)
    to_column = lambda z, y, x, c: (z, y, 1 - x, c)
    to_row = lambda z, y, x, c: (z, 1 - y, x, c)
    other_side = lambda z, y, x, c: (z, y, x, 1 - c)
    after = lambda array, *others: lax.optimization_barrier((array,) + others)[0]

    by_token = lambda a: jnp.swapaxes(a, 0, 1)
    payload, columns = prepare(
        by_token(hidden_states),
        jnp.swapaxes(routes, 1, 2),
        capacity,
        experts,
    )
    me = after(me, columns)
    z, y, x, side = place(me)
    token = np.arange(4 * block_rows)
    group = (token // block_rows * steps_total + token % steps_total) * 256
    group = jnp.asarray(group, jnp.float32)[None]
    slots = np.arange(2 * experts_local * 4 * slot_span).reshape(
        2, experts_local, 4, steps_total, capacity
    )
    of_side, of_expert, of_block, of_step, of_slot = [
        number.reshape(-1) for number in np.indices(slots.shape)
    ]
    wanted_expert = jnp.where(of_side == 0, me, me ^ 1) * experts_local + of_expert
    wanted = wanted_expert * capacity + of_slot + (of_block * steps_total + of_step) * 256
    wanted = jnp.broadcast_to(wanted.astype(jnp.float32)[:, None], (slots.size, LANES))

    planes = [z ^ offset for offset in range(lines)]
    if lines == 4:
        inner, beyond = (z == 1) | (z == 2), z // 2 * 2 ^ 2
        planes[2:] = [beyond + z // 2, beyond + 1 - z // 2]
    group_id = np.arange(peers)
    owners = device_at(
        jnp.stack(planes)[group_id // INNER],
        y ^ group_id // 2 % EDGE,
        x ^ group_id % EDGE,
        side ^ group_id // 4 % EDGE,
    ).astype(jnp.int32)

    blocks, keeps, cut = [], [], padded(block_rows // 2)

    def add_item(sources):
        keep, give = pick(sources, group, wanted, model_width)
        keeps.append(keep)
        blocks.extend([keep, send(give, other_side)])

    column, row = send(payload, to_column), send(payload, to_row)
    if lines == 4:
        middle = lambda z, y, x, c: (3 - z, y, x, c) if z in (1, 2) else None
        outward = lambda z, y, x, c: (z ^ 1, y, x, c) if z in (1, 2) else None
        next_line = send(payload, to_line(1))
        near_plane = send(after(payload, wanted), middle)
        far_plane = send(next_line, middle)
        near_out = send(near_plane, outward)
        far_out = send(far_plane, outward)
        halves = column[:cut], row[cut:]
        far = send(halves[0], to_row), send(halves[1], to_column)
        add_item([after(payload, far_plane), column, row, *far])
        own = after(next_line, *halves, owners)
        column, row = send(own, to_column), send(own, to_row)
        halves = column, row
        far = send(far[0], to_line(1)), send(far[1], to_line(1))
        add_item([own, column, row, *far])
        own = after(jnp.where(inner, near_plane, near_out), *halves)
        column, row = send(own, to_column), send(own, to_row)
        halves = column[:cut], row[cut:]
        past, far = far, (send(halves[0], to_row), send(halves[1], to_column))
        add_item([own, column, row, *far])
        own = after(jnp.where(inner, far_plane, far_out), *halves, *past, keeps[0])
        column, row = send(own, to_column), send(own, to_row)
        split = 2 * INNER
        early = run_experts(
            blocks[:4], owners[:split] % split, slot_span, gate_full, up_full
        )
        halves = lax.optimization_barrier((column[:cut], row[cut:], *far, early))[:2]
        far = send(halves[0], to_row), send(halves[1], to_column)
        add_item([own, column, row, *far])
    else:
        for offset in range(lines):
            own = send(payload, to_line(offset)) if offset else payload
            if offset:
                column, row = send(own, to_column), send(own, to_row)
            far = send(column[:cut], to_row), send(row[cut:], to_column)
            add_item([own, column, row, *far])
    if lines == 4:
        places = jnp.concatenate([owners[split:], (z // 2 * split)[None]])
        outgoing = run_experts(blocks[4:], places, slot_span, gate_full, up_full, early)
    else:
        outgoing = run_experts(blocks, owners, slot_span, gate_full, up_full)
    returned = lax.all_to_all(outgoing, "expert", split_axis=0, concat_axis=0, tiled=True)
    attn_out = attention(
        queries, new_keys, new_values, cache_keys, cache_values, after(lengths, outgoing)
    )
    back_rows = returned.reshape(experts * slot_span, hidden_width)
    moe_hidden = combine(
        back_rows, columns, by_token(gates).reshape(block_rows, TOPK), local_rows, steps_total
    )
    return (by_token(moe_hidden), attn_out)


def solution(mesh):
    in_specs = (
        P(None, ("replica", "expert"), None),
        P(None, ("replica", "expert"), None),
        P(None, ("replica", "expert"), None),
        P("expert", "replica", None),
        P("expert", "replica", None),
        P(None, ("replica", "expert"), None),
        P(None, ("replica", "expert"), None),
        P(None, ("replica", "expert"), None),
        P(("replica", "expert"), None, None),
        P(("replica", "expert"), None, None),
        P(("replica", "expert")),
    )
    out_specs = (P(None, ("replica", "expert"), None), P(None, ("replica", "expert"), None))
    return jax.shard_map(
        per_device, mesh=mesh, in_specs=in_specs, out_specs=out_specs, check_vma=False
    )
```

```python
import functools
import math

import jax
import jax.numpy as jnp
import numpy as np
from jax import lax
from jax.experimental import pallas as pl
from jax.experimental.pallas import tpu as pltpu
from jax.sharding import PartitionSpec as P

HQ = 64
KVH = 4
HD = 128
TOPK = 8
LANES = 128
EDGE = 2
INNER = EDGE**3
VMEM_BYTES = 50 * 1024 * 1024
EXPERT_VMEM = 50 * 1024 * 1024


def attention_kernel(lengths_ref, q_ref, nk_ref, nv_ref, k_ref, v_ref, out_ref, *, groups):
    rows, steps, _ = q_ref.shape
    cache = k_ref.shape[1]
    extra = 16
    many = steps*groups
    scale = 1.0/math.sqrt(HD)
    shape = (cache+extra, 2*many)
    position = lax.broadcasted_iota(jnp.int32, shape, 0)
    step = lax.broadcasted_iota(jnp.int32, shape, 1) % steps
    first = pl.program_id(0)*rows
    pad = jnp.zeros((extra-steps, 2*HD), jnp.float32)
    none = jnp.zeros((many, HD), jnp.float32)
    for r in range(rows):
        limit = jnp.where(position < cache, lengths_ref[first + r], step + (cache + 1))
        valid = position < limit
        for pair in range(KVH//2):
            wide = pl.ds(pair*2*HD, 2*HD)
            def with_new(cached, new):
                fresh = jnp.concatenate([new[r, :, wide].astype(jnp.float32), pad], axis=0)
                return jnp.concatenate([cached[r, :, wide], fresh.astype(jnp.bfloat16)], axis=0)
            heads = [q_ref[r, :, (pair*2*groups+h)*HD:(pair*2*groups+h+1)*HD].astype(jnp.float32) for h in range(2*groups)]
            low = jnp.concatenate(heads[:groups], axis=0)
            high = jnp.concatenate(heads[groups:], axis=0)
            asked = jnp.concatenate([jnp.concatenate([low, none], axis=1), jnp.concatenate([none, high], axis=1)], axis=0).astype(jnp.bfloat16)
            scores = lax.dot_general(with_new(k_ref, nk_ref), asked, (((1,),(1,)),((),())), preferred_element_type=jnp.float32)*scale
            scores = jnp.where(valid, scores, -jnp.inf)
            weights = jnp.exp(scores - jnp.max(scores, axis=0, keepdims=True))
            probs = (weights * (1.0/jnp.sum(weights, axis=0, keepdims=True))).astype(jnp.bfloat16)
            mixed = lax.dot_general(probs, with_new(v_ref, nv_ref), (((0,),(0,)),((),())), preferred_element_type=jnp.float32)
            for h in range(2*groups):
                at = h//groups*HD
                out_ref[r, :, (pair*2*groups+h)*HD:(pair*2*groups+h+1)*HD] = mixed[h*steps:(h+1)*steps, at:at+HD].astype(out_ref.dtype)

def attention(queries,new_keys,new_values,cache_keys,cache_values,lengths):
    steps, rows, _ = queries.shape
    groups = HQ//KVH
    cache = cache_keys.shape[1]
    part = max(n for n in range(1,8) if rows % n == 0)
    turn = lambda a: jnp.swapaxes(a,0,1)
    spec = lambda a: pl.BlockSpec((part,)+a.shape[1:], lambda i:(i,0,0))
    arrays = (turn(queries), turn(new_keys), turn(new_values), cache_keys, cache_values)
    out= pl.pallas_call(
        functools.partial(attention_kernel, groups=groups),
        grid=(rows//part,),
        in_specs=[pl.BlockSpec(memory_space=pltpu.SMEM)]+[spec(a) for a in arrays],
        out_specs=spec(arrays[0]),
        out_shape=jax.ShapeDtypeStruct(arrays[0].shape, queries.dtype),
        compiler_params=pltpu.CompilerParams(vmem_limit_bytes=16 * 1024 * 1024),
        name="attention",
    )(lengths, *arrays)
    return turn(out)


def place(index):
    return index // INNER, index // 4 % EDGE, index // 2 % EDGE, index % EDGE


def device_at(line, row, column, side):
    return ((line * EDGE + row) * EDGE + column) * EDGE + side


def moves(peers, target):
    pairs = [(index, target(*place(index))) for index in range(peers)]
    return [(index, device_at(*to)) for index, to in pairs if to is not None]


def padded(rows):
    return -(-rows // 16) * 16


def prepare_kernel(states_ref, routes_ref, payload_ref, columns_ref, *, capacity, experts):
    tokens, steps, width = states_ref.shape
    states = jnp.concatenate(
        [states_ref[token].astype(jnp.float32) for token in range(tokens)], axis=0
    )
    scale = lax.rsqrt(jnp.mean(states * states, axis=-1, keepdims=True) + 1e-06)
    payload_ref[:, :width] = (states * scale).astype(payload_ref.dtype)
    rows = tokens * steps
    row_ids = lax.broadcasted_iota(jnp.int32, (rows, tokens), 0)
    row_tokens = row_ids // steps == lax.broadcasted_iota(jnp.int32, (rows, tokens), 1)
    routes = sum(
        lax.dot_general(
            (row_tokens & (row_ids % steps == step)).astype(jnp.float32).astype(jnp.bfloat16),
            routes_ref[step].astype(jnp.float32).astype(jnp.bfloat16),
            (((1,), (1,)), ((), ())),
            preferred_element_type=jnp.float32,
        )
        for step in range(steps)
    ).astype(jnp.int32)
    first = lax.broadcasted_iota(jnp.int32, (rows, rows), 0)
    second = lax.broadcasted_iota(jnp.int32, (rows, rows), 1)
    order = ((first % steps == second % steps) & (first > second)).astype(jnp.float32)
    expert_ids = lax.broadcasted_iota(jnp.int32, (rows, experts), 1)
    marks = [
        (routes[:, choice : choice + 1] == expert_ids).astype(jnp.float32)
        for choice in range(TOPK)
    ]
    named = sum(marks)
    earlier = jnp.dot(
        order.astype(jnp.bfloat16), named.astype(jnp.bfloat16), preferred_element_type=jnp.float32
    )
    lane_ids = lax.broadcasted_iota(jnp.int32, (rows, LANES), 1)
    step = lax.broadcasted_iota(jnp.int32, (rows, 1), 0) % steps
    codes = jnp.zeros((rows, LANES), jnp.float32)
    columns = jnp.zeros((rows, LANES), jnp.int32)
    for choice in range(TOPK):
        slot = jnp.sum(earlier * marks[choice], axis=-1, keepdims=True)
        expert = routes[:, choice : choice + 1]
        code = expert.astype(jnp.float32) * capacity + slot
        codes = jnp.where(lane_ids == choice, code, codes)
        column = (expert * steps + step) * capacity + slot.astype(jnp.int32)
        columns = jnp.where(lane_ids == choice, column, columns)
    payload_ref[:, width:] = codes.astype(payload_ref.dtype)
    columns_ref[...] = columns


def prepare(states, routes, capacity, experts):
    tokens, steps, width = states.shape
    rows = tokens * steps
    return pl.pallas_call(
        functools.partial(prepare_kernel, capacity=capacity, experts=experts),
        out_shape=(
            jax.ShapeDtypeStruct((rows, width + LANES), jnp.bfloat16),
            jax.ShapeDtypeStruct((rows, LANES), jnp.int32),
        ),
        compiler_params=pltpu.CompilerParams(vmem_limit_bytes=VMEM_BYTES),
        name="prepare",
    )(states, routes)


def pick_kernel(*refs, parts):
    sources, codes_refs = refs[:parts], refs[parts : 2 * parts]
    group_ref, wanted_ref, keep_ref, send_ref, onehot_ref = refs[2 * parts :]

    @pl.when(pl.program_id(0) == 0)
    def _():
        codes = jnp.concatenate([ref[...].astype(jnp.float32) for ref in codes_refs], axis=0).T
        wanted, group = wanted_ref[:, :1], group_ref[...]
        hits = jnp.zeros((wanted.shape[0], group.shape[1]), jnp.float32)
        for choice in range(TOPK):
            hits = jnp.where(codes[choice : choice + 1] + group == wanted, 1.0, hits)
        onehot_ref[...] = hits.astype(jnp.bfloat16)

    rows = jnp.concatenate([ref[...] for ref in sources], axis=0)
    kept = keep_ref.shape[0]
    picked = jnp.dot(onehot_ref[...], rows, preferred_element_type=jnp.float32)
    picked = picked.astype(keep_ref.dtype)
    keep_ref[...] = picked[:kept]
    send_ref[...] = picked[kept:]


def pick(sources, group, wanted, width):
    rows, slots = group.shape[1], wanted.shape[0]
    cuts = 4 if width % (4 * LANES) == 0 else 1
    block = width // cuts
    sources = [source if isinstance(source, tuple) else (source, 0, 1) for source in sources]
    arrays = [source[0] for source in sources]
    piece = lambda a, n, of: pl.BlockSpec((a.shape[0] // of, block), lambda i: (n, i))
    codes = lambda a, n, of: pl.BlockSpec((a.shape[0] // of, LANES), lambda i: (n, width // LANES))
    whole = lambda a: pl.BlockSpec(a.shape, lambda i: (0, 0))
    return pl.pallas_call(
        functools.partial(pick_kernel, parts=len(sources)),
        grid=(cuts,),
        in_specs=[piece(*source) for source in sources]
        + [codes(*source) for source in sources]
        + [whole(group), whole(wanted)],
        out_specs=[pl.BlockSpec((slots // 2, block), lambda i: (0, i))] * 2,
        out_shape=[jax.ShapeDtypeStruct((slots // 2, width), jnp.bfloat16)] * 2,
        scratch_shapes=[pltpu.VMEM((slots, rows), jnp.bfloat16)],
        compiler_params=pltpu.CompilerParams(vmem_limit_bytes=VMEM_BYTES),
        name="pick",
    )(*arrays, *arrays, group, wanted)


def expert_kernel(owners_ref, *refs, count, part, earlier):
    x_refs, refs = refs[:count], refs[count:]
    done_ref, refs = (refs[0], refs[1:]) if earlier else (None, refs)
    gate_ref, up_ref, out_ref, rows_ref, arrived = refs
    hidden_part, expert = pl.program_id(0), pl.program_id(1)
    experts_local = rows_ref.shape[0]
    span = out_ref.shape[1] // experts_local

    def copy(number, which):
        return pltpu.make_async_copy(
            x_refs[number].at[pl.ds(which * part, part)],
            rows_ref.at[which, pl.ds(number * part, part)],
            arrived.at[which, number],
        )

    @pl.when((hidden_part == 0) & (expert == 0))
    def _():
        for which in range(experts_local):
            for number in range(count):
                copy(number, which).start()

    for which in range(experts_local):

        @pl.when((hidden_part == 0) & (expert == which))
        def _():
            for number in range(count):
                copy(number, which).wait()

    if earlier:

        @pl.when(expert == 0)
        def _():
            first = owners_ref[owners_ref.shape[0] - 1]
            out_ref[pl.ds(first, done_ref.shape[0])] = done_ref[...]

    rows = rows_ref[expert]
    gate = jnp.dot(rows, gate_ref[0], preferred_element_type=jnp.float32)
    up = jnp.dot(rows, up_ref[0], preferred_element_type=jnp.float32)
    inner = (gate / (1.0 + jnp.exp(-gate)) * up).astype(out_ref.dtype)
    for which in range(experts_local):

        @pl.when(expert == which)
        def _():
            for group in range(rows_ref.shape[1] // span):
                out_ref[owners_ref[group], which * span : (which + 1) * span, :] = inner[
                    group * span : (group + 1) * span
                ]


def run_experts(arrays, owners, span, w_gate, w_up, earlier=None):
    experts_local, width, hidden = w_gate.shape
    part, count = arrays[0].shape[0] // experts_local, len(arrays)
    rows = count * part
    block = 2 * LANES
    done = [] if earlier is None else [earlier]
    places = rows // span + sum(a.shape[0] for a in done)
    return pl.pallas_call(
        functools.partial(
            expert_kernel, count=count, part=part, earlier=earlier is not None
        ),
        grid=(hidden // block, experts_local),
        in_specs=[pl.BlockSpec(memory_space=pltpu.SMEM)]
        + [pl.BlockSpec(memory_space=pl.ANY)] * count
        + [pl.BlockSpec(a.shape[:2] + (block,), lambda f, e: (0, 0, f)) for a in done]
        + [pl.BlockSpec((1, width, block), lambda f, e: (e, 0, f))] * 2,
        out_specs=pl.BlockSpec(
            (places, experts_local * span, block), lambda f, e: (0, 0, f)
        ),
        out_shape=jax.ShapeDtypeStruct(
            (places, experts_local * span, hidden), jnp.bfloat16
        ),
        scratch_shapes=[
            pltpu.VMEM((experts_local, rows, width), jnp.bfloat16),
            pltpu.SemaphoreType.DMA((experts_local, count)),
        ],
        compiler_params=pltpu.CompilerParams(vmem_limit_bytes=EXPERT_VMEM),
        name="experts",
    )(owners, *arrays, *done, w_gate, w_up)


def combine_kernel(back_ref, columns_ref, gates_ref, out_ref):
    tokens, steps, _ = out_ref.shape
    rows = tokens * steps
    slots, hidden = back_ref.shape
    gates = gates_ref[...]
    mixing = gates / jnp.sum(gates, axis=-1, keepdims=True)
    ids = lax.broadcasted_iota(jnp.int32, (rows, slots), 1)
    marks = [
        (columns_ref[:, choice : choice + 1] == ids).astype(jnp.float32) for choice in range(TOPK)
    ]
    picked = jnp.dot(
        jnp.concatenate(marks, axis=0).astype(jnp.bfloat16),
        back_ref[...],
        preferred_element_type=jnp.float32,
    )
    for choice in range(TOPK):
        scaled = picked[choice * rows : (choice + 1) * rows] * mixing[:, choice : choice + 1]
        scaled = scaled.astype(out_ref.dtype)
        for token in range(tokens):
            out_ref[token, :, choice * hidden : (choice + 1) * hidden] = scaled[
                token * steps : (token + 1) * steps
            ]


def combine(back, columns, gates, tokens, steps):
    return pl.pallas_call(
        combine_kernel,
        out_shape=jax.ShapeDtypeStruct((tokens, steps, TOPK * back.shape[1]), jnp.bfloat16),
        compiler_params=pltpu.CompilerParams(vmem_limit_bytes=12 * 1024 * 1024),
        name="combine",
    )(back, columns, gates)


def per_device(
    hidden_states,
    routes,
    gates,
    w_gate,
    w_up,
    queries,
    new_keys,
    new_values,
    cache_keys,
    cache_values,
    lengths,
):
    peers = lax.axis_size("expert")
    me = lax.axis_index("expert")
    lines = peers // INNER
    experts_local = w_gate.shape[0]
    experts = experts_local * peers
    steps_total, local_rows, model_width = hidden_states.shape
    capacity = local_rows * TOPK * 2 // experts
    slot_span = steps_total * capacity
    gate_full, up_full = (
        lax.all_gather(w_gate, "replica", axis=1, tiled=True),
        lax.all_gather(w_up, "replica", axis=1, tiled=True),
    )
    hidden_width = gate_full.shape[2]
    block_rows = steps_total * local_rows

    assert experts * capacity <= 256
    send = lambda array, target: lax.ppermute(array, "expert", moves(peers, target))
    to_line = lambda offset: lambda z, y, x, c: (z ^ offset, y, x, c)
    to_column = lambda z, y, x, c: (z, y, 1 - x, c)
    to_row = lambda z, y, x, c: (z, 1 - y, x, c)
    other_side = lambda z, y, x, c: (z, y, x, 1 - c)
    after = lambda array, *others: lax.optimization_barrier((array,) + others)[0]

    by_token = lambda a: jnp.swapaxes(a, 0, 1)
    payload, columns = prepare(
        by_token(hidden_states),
        jnp.swapaxes(routes, 1, 2),
        capacity,
        experts,
    )
    me = after(me, columns)
    z, y, x, side = place(me)
    token = np.arange(4 * block_rows)
    group = (token // block_rows * steps_total + token % steps_total) * 256
    group = jnp.asarray(group, jnp.float32)[None]
    slots = np.arange(2 * experts_local * 4 * slot_span).reshape(
        2, experts_local, 4, steps_total, capacity
    )
    of_side, of_expert, of_block, of_step, of_slot = [
        number.reshape(-1) for number in np.indices(slots.shape)
    ]
    wanted_expert = jnp.where(of_side == 0, me, me ^ 1) * experts_local + of_expert
    wanted = wanted_expert * capacity + of_slot + (of_block * steps_total + of_step) * 256
    wanted = jnp.broadcast_to(wanted.astype(jnp.float32)[:, None], (slots.size, LANES))

    planes = [z ^ offset for offset in range(lines)]
    if lines == 4:
        inner, beyond = (z == 1) | (z == 2), z // 2 * 2 ^ 2
        planes[2:] = [beyond + z // 2, beyond + 1 - z // 2]
    group_id = np.arange(peers)
    owners = device_at(
        jnp.stack(planes)[group_id // INNER],
        y ^ group_id // 2 % EDGE,
        x ^ group_id % EDGE,
        side ^ group_id // 4 % EDGE,
    ).astype(jnp.int32)

    blocks, keeps, cut = [], [], padded(block_rows // 2)

    def add_item(sources):
        keep, give = pick(sources, group, wanted, model_width)
        keeps.append(keep)
        blocks.extend([keep, send(give, other_side)])

    column, row = send(payload, to_column), send(payload, to_row)
    if lines == 4:
        middle = lambda z, y, x, c: (3 - z, y, x, c) if z in (1, 2) else None
        outward = lambda z, y, x, c: (z ^ 1, y, x, c) if z in (1, 2) else None
        next_line = send(payload, to_line(1))
        near_plane = send(after(payload, wanted), middle)
        far_plane = send(next_line, middle)
        near_out = send(near_plane, outward)
        far_out = send(far_plane, outward)
        halves = column[:cut], row[cut:]
        far = send(halves[0], to_row), send(halves[1], to_column)
        add_item([after(payload, far_plane), column, row, *far])
        own = after(next_line, *halves, owners)
        column, row = send(own, to_column), send(own, to_row)
        halves = column, row
        far = send(far[0], to_line(1)), send(far[1], to_line(1))
        add_item([own, column, row, *far])
        own = after(jnp.where(inner, near_plane, near_out), *halves)
        column, row = send(own, to_column), send(own, to_row)
        halves = column[:cut], row[cut:]
        past, far = far, (send(halves[0], to_row), send(halves[1], to_column))
        add_item([own, column, row, *far])
        own = after(jnp.where(inner, far_plane, far_out), *halves, *past, keeps[0])
        column, row = send(own, to_column), send(own, to_row)
        split = 2 * INNER
        early = run_experts(
            blocks[:4], owners[:split] % split, slot_span, gate_full, up_full
        )
        halves = lax.optimization_barrier((column[:cut], row[cut:], *far, early))[:2]
        far = send(halves[0], to_row), send(halves[1], to_column)
        add_item([own, column, row, *far])
    else:
        for offset in range(lines):
            own = send(payload, to_line(offset)) if offset else payload
            if offset:
                column, row = send(own, to_column), send(own, to_row)
            far = send(column[:cut], to_row), send(row[cut:], to_column)
            add_item([own, column, row, *far])
    if lines == 4:
        places = jnp.concatenate([owners[split:], (z // 2 * split)[None]])
        outgoing = run_experts(blocks[4:], places, slot_span, gate_full, up_full, early)
    else:
        outgoing = run_experts(blocks, owners, slot_span, gate_full, up_full)
    returned = lax.all_to_all(outgoing, "expert", split_axis=0, concat_axis=0, tiled=True)
    attn_out = attention(
        queries, new_keys, new_values, cache_keys, cache_values, after(lengths, outgoing)
    )
    back_rows = returned.reshape(experts * slot_span, hidden_width)
    moe_hidden = combine(
        back_rows, columns, by_token(gates).reshape(block_rows, TOPK), local_rows, steps_total
    )
    return (by_token(moe_hidden), attn_out)


def solution(mesh):
    in_specs = (
        P(None, ("replica", "expert"), None),
        P(None, ("replica", "expert"), None),
        P(None, ("replica", "expert"), None),
        P("expert", "replica", None),
        P("expert", "replica", None),
        P(None, ("replica", "expert"), None),
        P(None, ("replica", "expert"), None),
        P(None, ("replica", "expert"), None),
        P(("replica", "expert"), None, None),
        P(("replica", "expert"), None, None),
        P(("replica", "expert")),
    )
    out_specs = (P(None, ("replica", "expert"), None), P(None, ("replica", "expert"), None))
    return jax.shard_map(
        per_device, mesh=mesh, in_specs=in_specs, out_specs=out_specs, check_vma=False
    )
```
